32 devices in a mesh: dp: 8 (over y, x, core), ctx: 4 (over z).
Axes of the slice: x: 2, y: 2, z: 4, core: 2. Of those that a mesh axis runs over, the one named last changes fastest.
Arguments:
- hidden: bfloat16 [8, 512, 4096], P('dp', 'ctx'), may hold values from -6 to 6
- dt_weight: bfloat16 [4096, 32], P('dp'), may hold values from -0.09375 to 0.09375
- ssm_input: bfloat16 [8, 512, 2048], P('dp', 'ctx'), may hold values from -6 to 6
- grad_output: bfloat16 [8, 512, 2048], P('dp', 'ctx'), may hold values from -1 to 1
- b_matrix: bfloat16 [8, 512, 1024], P('dp', 'ctx'), may hold values from -0.59765625 to 0.59765625
- c_matrix: bfloat16 [8, 512, 1024], P('dp', 'ctx'), may hold values from -0.59765625 to 0.59765625
- stored_states: bfloat16 [8, 4, 32, 64, 128], P('dp', 'ctx'), may hold values from -6 to 6
- step_bias: float32 [32], replicated, may hold values from -4 to 0.5
- decay_code: int32 [32], replicated, may hold values from 16 to 15872
- head_group: int32 [32], replicated, may hold values from 0 to 7
Outputs:
- grad_b: bfloat16 [8, 512, 1024], P('dp', 'ctx')
- grad_w: float32 [4096, 32], P('dp')
The draws below stay inside these ranges and needn't reach their ends.
All inputs are finite; a program needn't handle non-finite values.
Results may differ from the reference program's by a relative error of at most 0.001.
Values may be sent and summed in bfloat16 or wider, within the bound.
A program may use at most 128 MiB of HBM per device.

```python
import jax
import jax.numpy as jnp
from jax import lax

D = 4096
HEADS = 32
HEADDIM = 64
NSTATE = 128
GROUPS = 8
BATCH = 8
SEQLEN = 512
N_CTX = 4


def draw_decay_code(key, part):
    key = jax.random.fold_in(key, 11)
    first_key, second_key, third_key = jax.random.split(key, 3)
    exponent = jax.random.randint(first_key, (HEADS,), 0, 10)
    mantissa = jax.random.randint(second_key, (HEADS,), 16, 32)
    codes = jnp.left_shift(mantissa, exponent).astype(jnp.int32)
    chosen = jax.random.permutation(third_key, HEADS)
    codes = codes.at[chosen[0]].set(15872)
    codes = codes.at[chosen[1]].set(16)
    return codes.astype(jnp.int32)


def draw_step_bias(key, part):
    key = jax.random.fold_in(key, 12)
    return jax.random.uniform(key, (HEADS,), jnp.float32, -3.0, 0.5)


def plant(drawn, rng, low, high):
    spot = [jax.random.randint(jax.random.fold_in(rng, axis), (), 0, length) for axis, length in enumerate(drawn.shape)]
    longest = drawn.shape.index(max(drawn.shape))
    neighbour = spot[:longest] + [(spot[longest] + 1) % drawn.shape[longest]] + spot[longest + 1:]
    return drawn.at[tuple(spot)].set(low).at[tuple(neighbour)].set(high)


def with_spikes(values, stream_key, source, target, shards_of, factor):
    owner, partner = [(jnp.arange(values.shape[dim]) // (values.shape[dim] // shards_of)).reshape([-1 if axis == dim else 1 for axis in range(values.ndim)]) for dim in (source, target)]
    chosen = jax.random.permutation(stream_key, shards_of)[partner]
    strong = (owner == chosen) | (owner == (partner + shards_of // 2) % shards_of)
    return jnp.where(strong, factor * values, values)


def steps_of(own_key, extent, shards, smallest, high):
    def one(axis_at, blocks):
        draws = jax.random.uniform(jax.random.fold_in(jax.random.fold_in(own_key, 6), axis_at), (blocks,), jnp.float32, smallest / len(shards), high / len(shards))
        return jnp.repeat(jnp.exp(draws), extent[axis_at] // blocks).reshape((-1,) + (1,) * (len(extent) - axis_at - 1))

    factor_of = one(*shards[0])
    for cut in shards[1:]:
        factor_of = factor_of * one(*cut)
    return factor_of


def normal_values(own_key, extent, scale, most, cuts=(), held_as=jnp.bfloat16):
    factor_of = steps_of(own_key, extent, cuts, -0.22, 0.18) if cuts else 1.0
    array = jax.random.normal(own_key, extent, jnp.float32) * scale * factor_of
    return jnp.minimum(jnp.maximum(array, -most), most).astype(held_as)


def gaussian_with(key, dims, width, reach, cuts, heavy, held_as=jnp.bfloat16):
    drawn = width * jax.random.normal(key, dims, jnp.float32)
    if cuts:
        drawn = drawn * steps_of(key, dims, cuts, -0.22, 0.18)
    return jnp.clip(with_spikes(drawn, jax.random.fold_in(key, 3), *heavy), -reach, reach).astype(held_as)


def setup_inputs(seed: int = 0) -> dict:
    arg_keys = jax.random.split(jax.random.key(seed), 11)
    return {
        "hidden": gaussian_with(arg_keys[0], (BATCH, SEQLEN, D), 1.0, 6.0, ((0, 8), (1, 4)), (0, 2, 8, 2.0)),
        "dt_weight": normal_values(arg_keys[1], (D, HEADS), D ** -0.5, 0.09375, ((0, 8),)),
        "ssm_input": normal_values(arg_keys[2], (BATCH, SEQLEN, HEADS * HEADDIM), 1.0, 6.0, ((0, 8), (1, 4))),
        "grad_output": normal_values(arg_keys[3], (BATCH, SEQLEN, HEADS * HEADDIM), 0.125, 1.0, ((0, 8), (1, 4))),
        "b_matrix": normal_values(arg_keys[4], (BATCH, SEQLEN, GROUPS * NSTATE), 0.09, 0.59765625, ((0, 8), (1, 4))),
        "c_matrix": normal_values(arg_keys[5], (BATCH, SEQLEN, GROUPS * NSTATE), 0.09, 0.59765625, ((0, 8), (1, 4))),
        "stored_states": normal_values(arg_keys[6], (BATCH, N_CTX, HEADS, HEADDIM, NSTATE), 1.0, 6.0, ((0, 8), (1, 4))),
        "step_bias": draw_step_bias(jax.random.fold_in(arg_keys[10], 71), 0),
        "decay_code": draw_decay_code(jax.random.fold_in(arg_keys[10], 71), 0),
        "head_group": plant(jax.random.randint(arg_keys[9], (HEADS,), 0, GROUPS), jax.random.fold_in(arg_keys[9], 1), 0, GROUPS - 1).astype(jnp.int32),
    }


exact_precision = lax.Precision.HIGHEST

def block_loss(projected, b_block, c_block, x_block, cot_block, start_state, step_bias, decay_rate, onehot):
    timestep = jax.nn.softplus(projected + step_bias[None, :])
    cumulative = jnp.cumsum(-decay_rate[None, :] * timestep, axis=0)
    b_heads = jnp.einsum('lgn,hg->lhn', b_block, onehot, precision=exact_precision)
    c_heads = jnp.einsum('lgn,hg->lhn', c_block, onehot, precision=exact_precision)
    scores = jnp.einsum('ihn,jhn->hij', c_heads, b_heads, precision=exact_precision)
    positions = jnp.arange(projected.shape[0])
    causal = (positions[:, None] >= positions[None, :])[None, :, :]
    log_gaps = cumulative.T[:, :, None] - cumulative.T[:, None, :]
    decay = jnp.where(causal, jnp.exp(jnp.where(causal, log_gaps, 0.0)), 0.0)
    weights = decay * scores * timestep.T[:, None, :]
    inner = jnp.einsum('hij,jhp->ihp', weights, x_block, precision=exact_precision)
    carried = jnp.exp(cumulative)[:, :, None] * jnp.einsum('hpn,ihn->ihp', start_state, c_heads, precision=exact_precision)
    output = inner + carried
    to_end = jnp.exp(cumulative[-1][None, :] - cumulative) * timestep
    final_state = jnp.exp(cumulative[-1])[:, None, None] * start_state + jnp.einsum('jh,jhp,jhn->hpn', to_end, x_block, b_heads, precision=exact_precision)
    return (jnp.sum(cot_block * output), final_state)

def sequence_loss(projected, b_rows, c_rows, x_rows, cot_rows, stored, step_bias, decay_rate, onehot):
    blocks = stored.shape[0]
    full_length = projected.shape[0]
    length = full_length // blocks
    heads_here = projected.shape[1]

    def advance(previous, sequence_items):
        proj_block, b_block, c_block, x_block, cot_block, state_block = sequence_items
        start_state = state_block + (previous - lax.stop_gradient(previous))
        block_value, final_state = block_loss(proj_block, b_block, c_block, x_block, cot_block, start_state, step_bias, decay_rate, onehot)
        return (final_state, block_value)
    sequence_items = (projected.reshape(blocks, length, heads_here), b_rows.reshape(blocks, length, b_rows.shape[1], b_rows.shape[2]), c_rows.reshape(blocks, length, c_rows.shape[1], c_rows.shape[2]), x_rows.reshape(blocks, length, x_rows.shape[1], x_rows.shape[2]), cot_rows.reshape(blocks, length, cot_rows.shape[1], cot_rows.shape[2]), stored)
    zero_start = jnp.zeros(stored.shape[1:], jnp.float32)
    _, block_values = lax.scan(advance, zero_start, sequence_items)
    return jnp.sum(block_values)

def reference(hidden, dt_weight, ssm_input, grad_output, b_matrix, c_matrix, stored_states, step_bias, decay_code, head_group):
    full_length = hidden.shape[1]
    head_count = step_bias.shape[0]
    decay_rate = decay_code.astype(jnp.float32) / (256.0 * full_length)
    onehot = (head_group[:, None] == jnp.arange(GROUPS, dtype=jnp.int32)[None, :]).astype(jnp.float32)
    weight_full = dt_weight.astype(jnp.float32)

    def per_sequence(sequence_items):
        hidden_rows, x_rows, cot_rows, b_rows, c_rows, stored = sequence_items
        hidden_full = hidden_rows.astype(jnp.float32)
        projected = jnp.dot(hidden_full, weight_full, precision=exact_precision)
        b_full = b_rows.astype(jnp.float32).reshape(full_length, GROUPS, NSTATE)
        c_full = c_rows.astype(jnp.float32).reshape(full_length, GROUPS, NSTATE)
        x_full = x_rows.astype(jnp.float32).reshape(full_length, head_count, HEADDIM)
        cot_full = cot_rows.astype(jnp.float32).reshape(full_length, head_count, HEADDIM)
        stored_full = stored.astype(jnp.float32)

        def loss_of(proj_arg, b_arg):
            return sequence_loss(proj_arg, b_arg, c_full, x_full, cot_full, stored_full, step_bias, decay_rate, onehot)
        _, pullback = jax.vjp(loss_of, projected, b_full)
        grad_projected, grad_keys = pullback(jnp.ones((), jnp.float32))
        grad_weight = jnp.dot(hidden_full.T, grad_projected, precision=exact_precision)
        return (grad_keys.reshape(full_length, GROUPS * NSTATE).astype(jnp.bfloat16), grad_weight)
    grads_b, grads_w = lax.map(per_sequence, (hidden, ssm_input, grad_output, b_matrix, c_matrix, stored_states))
    return (grads_b, lax.optimization_barrier(jnp.sum(grads_w, axis=0)))
```

```python
import functools

import jax
import jax.numpy as jnp
from jax import lax
from jax.experimental import pallas as pl
from jax.experimental.pallas import tpu as pltpu
from jax.sharding import PartitionSpec as P

HEADDIM = 64
NSTATE = 128
GROUPS = 8
CHUNK_HEADS = 4
FUSE_END = True

f32, bf16 = jnp.float32, jnp.bfloat16
MESH = pl.DeviceIdType.MESH
exact = lax.Precision.HIGHEST


def mm(a, b):
    return jnp.dot(a, b, preferred_element_type=f32)


def mm_nt(a, b):
    return lax.dot_general(a, b, (((1,), (1,)), ((), ())), preferred_element_type=f32)


def split(v):
    hi = v.astype(bf16)
    return hi, (v - hi.astype(f32)).astype(bf16)


def kernel(cfg, hid, w, x, cot, b, c, st, bias, code, hg, *rest):
    n_dp, n_ctx, gather, fuse = cfg
    (out_b, out_w), rest = rest[:2], rest[2:]
    (wall, cot_t, bg, cg2, sc, cum_s, last_s, growth_s, elast_s, cumb, stepb, acc,
     row_s, col_s, car_s, end_s, gs_s, send_s, recv_s, w_own,
     w_send, w_recv, ch_send, ch_recv) = rest[:24]
    length = x.shape[0]
    heads = bias.shape[1]
    depth = hid.shape[1] // n_dp
    full_length = length * n_ctx
    dp = lax.axis_index("dp")
    ctx = lax.axis_index("ctx")
    is_last = ctx == n_ctx - 1

    if fuse:
        hall, graw_own, graw_all, part, h_send, h_recv, g_send, g_recv, p_all, p_send, p_recv = rest[24:]

    barrier = pltpu.get_barrier_semaphore()
    if gather or fuse:
        for r in range(1, n_dp):
            pl.semaphore_signal(barrier, inc=1, device_id=(lax.rem(dp + r, n_dp), ctx), device_id_type=MESH)
    for r in range(1, n_ctx):
        pl.semaphore_signal(barrier, inc=1, device_id=(dp, lax.rem(ctx + r, n_ctx)), device_id_type=MESH)

    ri = lax.broadcasted_iota(jnp.int32, (heads, heads), 0)
    ci = lax.broadcasted_iota(jnp.int32, (heads, heads), 1)
    eye = ri == ci
    if gather:
        w_own[...] = mm_nt(eye.astype(bf16), w[...]).astype(bf16)
    pl.semaphore_wait(barrier, (n_dp - 1 if gather or fuse else 0) + n_ctx - 1)

    def w_copy(r, peer, slot):
        return pltpu.make_async_remote_copy(
            src_ref=w_own, dst_ref=wall.at[slot], send_sem=w_send.at[r], recv_sem=w_recv.at[r],
            device_id=(peer, ctx), device_id_type=MESH)

    def h_copy(r, peer, slot):
        return pltpu.make_async_remote_copy(
            src_ref=hid.at[:, pl.ds(pl.multiple_of(peer * depth, depth), depth)], dst_ref=hall.at[slot],
            send_sem=h_send.at[r], recv_sem=h_recv.at[r], device_id=(peer, ctx), device_id_type=MESH)

    if gather:
        for r in range(1, n_dp):
            w_copy(r, lax.rem(dp + r, n_dp), dp).start()
        wall[dp] = w_own[...]
    if fuse:
        for r in range(1, n_dp):
            h_copy(r, lax.rem(dp + r, n_dp), dp).start()
        hall[dp] = hid[:, pl.ds(pl.multiple_of(dp * depth, depth), depth)]

    for k in range(x.shape[1] // 128):
        cot_t[pl.ds(128 * k, 128), :] = cot[:, pl.ds(128 * k, 128)].T
    for g in range(GROUPS):
        b_g = b[:, pl.ds(NSTATE * g, NSTATE)]
        c_g = c[:, pl.ds(NSTATE * g, NSTATE)]
        bg[g] = b_g.astype(f32)
        cg2[g, :length, :] = c_g
        cg2[g, length:, :] = c_g
        sc[g] = mm_nt(b_g, c_g)
    acc[...] = jnp.zeros_like(acc)

    @pl.when(is_last)
    def _():
        recv_s[...] = jnp.zeros_like(recv_s)

    bias_c = jnp.sum(jnp.where(eye, bias[...], 0.0), axis=1, keepdims=True)
    rate_c = jnp.sum(jnp.where(eye, code[...].astype(f32), 0.0), axis=1, keepdims=True) / (256.0 * full_length)

    if gather:
        for r in range(1, n_dp):
            w_copy(r, lax.rem(dp + r, n_dp), lax.rem(dp - r + n_dp, n_dp)).wait_recv()
    proj = jnp.zeros((heads, length), f32)
    for d in range(n_dp):
        proj = proj + mm_nt(wall[d] if gather else w[d], hid[:, d * depth:(d + 1) * depth])
    shifted = proj + bias_c
    timestep = jnp.maximum(shifted, 0.0) + jnp.log1p(jnp.exp(-jnp.abs(shifted)))
    gain = 1.0 / (1.0 + jnp.exp(-shifted))
    rows = lax.broadcasted_iota(jnp.int32, (length, length), 0)
    cols = lax.broadcasted_iota(jnp.int32, (length, length), 1)
    causal = rows <= cols
    cum = jnp.dot(-rate_c * timestep, causal.astype(f32), precision=exact, preferred_element_type=f32)
    last = jnp.broadcast_to(cum[:, length - 1:length], (heads, length))
    cum_s[...] = cum
    last_s[...] = last
    growth_s[...] = jnp.exp(cum)
    elast_s[...] = jnp.exp(last)

    def chain(k):
        span = pl.ds(pl.multiple_of(k * (CHUNK_HEADS * HEADDIM), CHUNK_HEADS * HEADDIM), CHUNK_HEADS * HEADDIM)
        return pltpu.make_async_remote_copy(
            src_ref=send_s.at[span], dst_ref=recv_s.at[span], send_sem=ch_send.at[k], recv_sem=ch_recv.at[k],
            device_id=(dp, lax.rem(ctx - 1 + n_ctx, n_ctx)), device_id_type=MESH)

    def own_chunk(k, carry):
        for e in range(CHUNK_HEADS):
            h = k * CHUNK_HEADS + e
            span = pl.ds(pl.multiple_of(h * HEADDIM, HEADDIM), HEADDIM)
            weighted = cot_t[span, :].astype(f32) * growth_s[pl.ds(h, 1), :]
            both = mm(jnp.concatenate(split(weighted), axis=0), cg2[hg[h], :length, :])
            send_s[span, :] = both[:HEADDIM] + both[HEADDIM:]

        @pl.when(is_last)
        def _():
            chain(k).start()

        return carry

    chunks = heads // CHUNK_HEADS
    lax.fori_loop(0, chunks, own_chunk, 0)

    both_t = jnp.concatenate([cum, timestep, jnp.zeros((length - 2 * heads, length), f32)], axis=0).T
    for h in range(heads):
        cumb[h] = jnp.broadcast_to(both_t[:, h:h + 1], (length, length))
        stepb[h] = jnp.broadcast_to(both_t[:, heads + h:heads + h + 1], (length, length))

    low_lanes = lax.broadcasted_iota(jnp.int32, (length, 128), 1) < HEADDIM
    ones = jnp.ones((8, 256), bf16)

    def main_chunk(k, carry):
        @pl.when(ctx < n_ctx - 1)
        def _():
            chain(k).wait_recv()

        @pl.when(jnp.logical_and(ctx < n_ctx - 1, ctx > 0))
        def _():
            for e in range(CHUNK_HEADS):
                h = k * CHUNK_HEADS + e
                span = pl.ds(pl.multiple_of(h * HEADDIM, HEADDIM), HEADDIM)
                send_s[span, :] = send_s[span, :] + elast_s[pl.ds(h, 1), :] * recv_s[span, :]
            chain(k).start()

        grads = []
        for q in range(CHUNK_HEADS // 2):
            pair = k * (CHUNK_HEADS // 2) + q
            lanes = pl.ds(pl.multiple_of(pair * 128, 128), 128)
            xp = x[:, lanes]
            cp = cot[:, lanes]
            incoming = recv_s[lanes, :]
            rhs = jnp.concatenate(split(incoming), axis=0)
            product_state = incoming * st[lanes, :].astype(f32)
            for e in range(2):
                h = pair * 2 + e
                g = hg[h]
                row = pl.ds(h, 1)
                span = pl.ds(pl.multiple_of(h * HEADDIM, HEADDIM), HEADDIM)
                mask = low_lanes if e == 0 else jnp.logical_not(low_lanes)
                xm = jnp.where(mask, xp, jnp.zeros_like(xp))
                c2 = cg2[g]
                cum_h = cumb[h]
                step_h = stepb[h]
                gaps = cum_s[row, :] - cum_h
                decay = jnp.where(causal, jnp.exp(jnp.where(causal, gaps, 0.0)), 0.0)
                m = decay * mm_nt(xm, cp)
                scored = m * sc[g]
                x_state = mm(jnp.concatenate([xm, xm], axis=1), rhs)
                to_end = jnp.exp(last_s[row, :] - cum_h)
                grads.append((h, step_h * (mm(jnp.concatenate(split(m), axis=1), c2) + to_end * x_state)))
                row_s[row, :] = jnp.sum(scored * step_h, axis=0, keepdims=True)
                col_s[row, :] = mm_nt(ones, jnp.concatenate(split(scored), axis=1))[:1]
                end_s[row, :] = mm_nt(ones, jnp.concatenate(split(x_state * bg[g]), axis=1))[:1]
                carried = mm_nt(st[span, :], c2[:length])
                car_s[row, :] = jnp.sum(cot_t[span, :].astype(f32) * carried, axis=0, keepdims=True)
                gs_s[row, :] = jnp.sum(
                    product_state[e * HEADDIM:(e + 1) * HEADDIM], axis=0, keepdims=True)
        for g in range(GROUPS):
            total = acc[g]
            for h, value in grads:
                total = total + jnp.where(hg[h] == g, 1.0, 0.0) * value
            acc[g] = total
        return carry

    lax.fori_loop(0, chunks, main_chunk, 0)

    col = col_s[...]
    end_plain = jnp.exp(last_s[...] - cum_s[...]) * end_s[...]
    end_term = end_plain * timestep
    grad_cum = row_s[...] - col * timestep + growth_s[...] * car_s[...] - end_term
    end_total = jnp.sum(end_term, axis=1, keepdims=True) + elast_s[:, :1] * jnp.sum(gs_s[...], axis=1, keepdims=True)
    lane = lax.broadcasted_iota(jnp.int32, (heads, length), 1)
    grad_cum = grad_cum + jnp.where(lane == length - 1, end_total, 0.0)
    backward = jnp.dot(grad_cum, (rows >= cols).astype(f32), precision=exact, preferred_element_type=f32)
    grad_raw = (col + end_plain - rate_c * backward) * gain

    def g_copy(r, peer, slot):
        return pltpu.make_async_remote_copy(
            src_ref=graw_own, dst_ref=graw_all.at[slot], send_sem=g_send.at[r], recv_sem=g_recv.at[r],
            device_id=(peer, ctx), device_id_type=MESH)

    def p_copy(r, peer, slot):
        return pltpu.make_async_remote_copy(
            src_ref=part, dst_ref=p_all.at[slot], send_sem=p_send.at[r], recv_sem=p_recv.at[r],
            device_id=(dp, peer), device_id_type=MESH)

    if fuse:
        graw_own[...] = grad_raw
        for r in range(1, n_dp):
            g_copy(r, lax.rem(dp + r, n_dp), dp).start()
        graw_all[dp] = grad_raw
    else:
        out_w[...] = grad_raw

    for g in range(GROUPS):
        out_b[:, pl.ds(NSTATE * g, NSTATE)] = acc[g].astype(bf16)

    if fuse:
        total = jnp.zeros((2 * heads, depth), f32)
        for r in range(1, n_dp):
            source = lax.rem(dp - r + n_dp, n_dp)
            h_copy(r, lax.rem(dp + r, n_dp), source).wait_recv()
        for r in range(1, n_dp):
            source = lax.rem(dp - r + n_dp, n_dp)
            g_copy(r, lax.rem(dp + r, n_dp), source).wait_recv()
        for d in range(n_dp):
            total = total + mm(jnp.concatenate(split(graw_all[d]), axis=0), hall[d])
        part[...] = total[:heads] + total[heads:]
        for r in range(1, n_ctx):
            p_copy(r, lax.rem(ctx + r, n_ctx), ctx).start()
        p_all[ctx] = part[...]
        for r in range(1, n_ctx):
            p_copy(r, lax.rem(ctx + r, n_ctx), lax.rem(ctx - r + n_ctx, n_ctx)).wait_recv()
        summed = p_all[0]
        for d in range(1, n_ctx):
            summed = summed + p_all[d]
        out_w[...] = summed
        for r in range(1, n_ctx):
            p_copy(r, lax.rem(ctx + r, n_ctx), ctx).wait_send()
        for r in range(1, n_dp):
            h_copy(r, lax.rem(dp + r, n_dp), dp).wait_send()
            g_copy(r, lax.rem(dp + r, n_dp), dp).wait_send()

    if gather:
        for r in range(1, n_dp):
            w_copy(r, lax.rem(dp + r, n_dp), dp).wait_send()

    @pl.when(ctx > 0)
    def _():
        def drain(k, carry):
            chain(k).wait_send()
            return carry

        lax.fori_loop(0, chunks, drain, 0)


def body(n_dp, n_ctx, hidden, dt_weight, ssm_input, grad_output, b_matrix, c_matrix,
         stored_states, step_bias, decay_code, head_group):
    length, width = hidden.shape[1:]
    depth = dt_weight.shape[0]
    heads = step_bias.shape[0]
    gather = depth % 128 == 0
    fuse = FUSE_END and gather
    hid = hidden[0]
    if gather:
        w = dt_weight
    else:
        w = lax.all_gather(dt_weight.T, "dp", axis=0, tiled=False)
    chunks = heads // CHUNK_HEADS
    vmem = pl.BlockSpec(memory_space=pltpu.VMEM)
    small = pltpu.VMEM((heads, length), f32)
    dma = pltpu.SemaphoreType.DMA
    scratch = [
        pltpu.VMEM((n_dp if gather else 1, heads, depth), bf16),
        pltpu.VMEM((heads * HEADDIM, length), bf16),
        pltpu.VMEM((GROUPS, length, NSTATE), f32),
        pltpu.VMEM((GROUPS, 2 * length, NSTATE), bf16),
        pltpu.VMEM((GROUPS, length, length), f32),
        small, small, small, small,
        pltpu.VMEM((heads, length, length), f32),
        pltpu.VMEM((heads, length, length), f32),
        pltpu.VMEM((GROUPS, length, NSTATE), f32),
        small, small, small, small, small,
        pltpu.VMEM((heads * HEADDIM, NSTATE), f32),
        pltpu.VMEM((heads * HEADDIM, NSTATE), f32),
        pltpu.VMEM((heads, depth), bf16),
        dma((n_dp,)), dma((n_dp,)), dma((chunks,)), dma((chunks,)),
    ]
    if fuse:
        scratch += [
            pltpu.VMEM((n_dp, length, depth), bf16),
            small,
            pltpu.VMEM((n_dp, heads, length), f32),
            pltpu.VMEM((heads, depth), f32),
            dma((n_dp,)), dma((n_dp,)), dma((n_dp,)), dma((n_dp,)),
            pltpu.VMEM((n_ctx, heads, depth), f32),
            dma((n_ctx,)), dma((n_ctx,)),
        ]
    grad_b, res = pl.pallas_call(
        functools.partial(kernel, (n_dp, n_ctx, gather, fuse)),
        out_shape=(
            jax.ShapeDtypeStruct((length, GROUPS * NSTATE), bf16),
            jax.ShapeDtypeStruct((heads, depth if fuse else length), f32),
        ),
        in_specs=[vmem] * 9 + [pl.BlockSpec(memory_space=pltpu.SMEM)],
        out_specs=(vmem, vmem),
        scratch_shapes=scratch,
        compiler_params=pltpu.CompilerParams(
            collective_id=0, has_side_effects=True, vmem_limit_bytes=48 * 1024 * 1024),
    )(hid, w, ssm_input[0], grad_output[0], b_matrix[0], c_matrix[0],
      stored_states.reshape(heads * HEADDIM, NSTATE), step_bias.reshape(1, heads),
      decay_code.reshape(1, heads), head_group)
    if fuse:
        grad_w = res.T
    else:
        hi = lax.reduce_precision(res, 8, 7)
        both = mm(jnp.concatenate([hi.astype(bf16), (res - hi).astype(bf16)], axis=0), hid)
        part = both[:heads] + both[heads:]
        part = lax.psum_scatter(part, "dp", scatter_dimension=1, tiled=True)
        grad_w = lax.psum(part, "ctx").T
    return grad_b[None], grad_w


def solution(mesh):
    return jax.shard_map(
        functools.partial(body, mesh.shape["dp"], mesh.shape["ctx"]),
        mesh=mesh,
        in_specs=(
            P("dp", "ctx", None),
            P("dp", None),
            P("dp", "ctx", None),
            P("dp", "ctx", None),
            P("dp", "ctx", None),
            P("dp", "ctx", None),
            P("dp", "ctx", None, None, None),
            P(),
            P(),
            P(),
        ),
        out_specs=(P("dp", "ctx", None), P("dp", None)),
        check_vma=False,
    )
```

```python
import functools

import jax
import jax.numpy as jnp
from jax import lax
from jax.experimental import pallas as pl
from jax.experimental.pallas import tpu as pltpu
from jax.sharding import PartitionSpec as P

HEADDIM = 64
NSTATE = 128
GROUPS = 8
CHUNK_HEADS = 4
FUSE_END = True

f32, bf16 = jnp.float32, jnp.bfloat16
MESH = pl.DeviceIdType.MESH
exact = lax.Precision.HIGHEST


def mm(a, b):
    return jnp.dot(a, b, preferred_element_type=f32)


def mm_nt(a, b):
    return lax.dot_general(a, b, (((1,), (1,)), ((), ())), preferred_element_type=f32)


def split(v):
    hi = v.astype(bf16)
    return hi, (v - hi.astype(f32)).astype(bf16)


def kernel(cfg, hid_h, w, x_h, cot_h, b_h, c_h, st_h, bias, code, hg, *rest):
    n_dp, n_ctx, gather, fuse = cfg
    (out_b, out_w), rest = rest[:2], rest[2:]
    (wall, cot_t, bg, cg2, sc, cum_s, last_s, growth_s, elast_s, cumb, stepb, acc,
     row_s, col_s, car_s, end_s, gs_s, send_s, recv_s, hid, x, cot, b, c, st, in_sem,
     w_send, w_recv, ch_send, ch_recv) = rest[:30]
    length = x.shape[0]
    heads = bias.shape[1]
    depth = hid.shape[1] // n_dp
    full_length = length * n_ctx
    dp = lax.axis_index("dp")
    ctx = lax.axis_index("ctx")
    is_last = ctx == n_ctx - 1

    if fuse:
        hall, graw_own, graw_all, part, h_send, h_recv, g_send, g_recv, p_all, p_send, p_recv = rest[30:]

    fetches = [
        pltpu.make_async_copy(source, target, in_sem.at[i])
        for i, (source, target) in enumerate(
            ((cot_h, cot), (c_h, c), (b_h, b), (hid_h, hid), (x_h, x), (st_h, st)))
    ]
    own_w = pltpu.make_async_copy(w, wall.at[dp if gather else 0], in_sem.at[6])
    barrier = pltpu.get_barrier_semaphore()
    if gather or fuse:
        for r in range(1, n_dp):
            pl.semaphore_signal(barrier, inc=1, device_id=(lax.rem(dp + r, n_dp), ctx), device_id_type=MESH)
    for r in range(1, n_ctx):
        pl.semaphore_signal(barrier, inc=1, device_id=(dp, lax.rem(ctx + r, n_ctx)), device_id_type=MESH)

    ri = lax.broadcasted_iota(jnp.int32, (heads, heads), 0)
    ci = lax.broadcasted_iota(jnp.int32, (heads, heads), 1)
    eye = ri == ci
    if gather:
        own_w.start()
    for fetch in fetches:
        fetch.start()
    pl.semaphore_wait(barrier, (n_dp - 1 if gather or fuse else 0) + n_ctx - 1)

    def w_copy(r, peer, slot):
        return pltpu.make_async_remote_copy(
            src_ref=w, dst_ref=wall.at[slot], send_sem=w_send.at[r], recv_sem=w_recv.at[r],
            device_id=(peer, ctx), device_id_type=MESH)

    def h_copy(r, peer, slot):
        return pltpu.make_async_remote_copy(
            src_ref=hid_h.at[:, pl.ds(pl.multiple_of(peer * depth, depth), depth)], dst_ref=hall.at[slot],
            send_sem=h_send.at[r], recv_sem=h_recv.at[r], device_id=(peer, ctx), device_id_type=MESH)

    if gather:
        for r in range(1, n_dp):
            w_copy(r, lax.rem(dp + r, n_dp), dp).start()
    if fuse:
        for r in range(1, n_dp):
            h_copy(r, lax.rem(dp + r, n_dp), dp).start()

    fetches[0].wait()
    for k in range(x.shape[1] // 128):
        cot_t[pl.ds(128 * k, 128), :] = cot[:, pl.ds(128 * k, 128)].T
    fetches[1].wait()
    fetches[2].wait()
    for g in range(GROUPS):
        b_g = b[:, pl.ds(NSTATE * g, NSTATE)]
        c_g = c[:, pl.ds(NSTATE * g, NSTATE)]
        bg[g] = b_g.astype(f32)
        cg2[g, :length, :] = c_g
        cg2[g, length:, :] = c_g
        sc[g] = mm_nt(b_g, c_g)
    acc[...] = jnp.zeros_like(acc)

    @pl.when(is_last)
    def _():
        recv_s[...] = jnp.zeros_like(recv_s)

    bias_c = jnp.sum(jnp.where(eye, bias[...], 0.0), axis=1, keepdims=True)
    rate_c = jnp.sum(jnp.where(eye, code[...].astype(f32), 0.0), axis=1, keepdims=True) / (256.0 * full_length)

    fetches[3].wait()
    if fuse:
        hall[dp] = hid[:, pl.ds(pl.multiple_of(dp * depth, depth), depth)]
    if gather:
        own_w.wait()
        for r in range(1, n_dp):
            w_copy(r, lax.rem(dp + r, n_dp), lax.rem(dp - r + n_dp, n_dp)).wait_recv()
    proj = jnp.zeros((heads, length), f32)
    for d in range(n_dp):
        proj = proj + mm_nt(wall[d] if gather else w[d], hid[:, d * depth:(d + 1) * depth])
    shifted = proj + bias_c
    timestep = jnp.maximum(shifted, 0.0) + jnp.log1p(jnp.exp(-jnp.abs(shifted)))
    gain = 1.0 / (1.0 + jnp.exp(-shifted))
    rows = lax.broadcasted_iota(jnp.int32, (length, length), 0)
    cols = lax.broadcasted_iota(jnp.int32, (length, length), 1)
    causal = rows <= cols
    cum = jnp.dot(-rate_c * timestep, causal.astype(f32), precision=exact, preferred_element_type=f32)
    last = jnp.broadcast_to(cum[:, length - 1:length], (heads, length))
    cum_s[...] = cum
    last_s[...] = last
    growth_s[...] = jnp.exp(cum)
    elast_s[...] = jnp.exp(last)

    def chain(k):
        span = pl.ds(pl.multiple_of(k * (CHUNK_HEADS * HEADDIM), CHUNK_HEADS * HEADDIM), CHUNK_HEADS * HEADDIM)
        return pltpu.make_async_remote_copy(
            src_ref=send_s.at[span], dst_ref=recv_s.at[span], send_sem=ch_send.at[k], recv_sem=ch_recv.at[k],
            device_id=(dp, lax.rem(ctx - 1 + n_ctx, n_ctx)), device_id_type=MESH)

    def own_chunk(k, carry):
        for e in range(CHUNK_HEADS):
            h = k * CHUNK_HEADS + e
            span = pl.ds(pl.multiple_of(h * HEADDIM, HEADDIM), HEADDIM)
            weighted = cot_t[span, :].astype(f32) * growth_s[pl.ds(h, 1), :]
            both = mm(jnp.concatenate(split(weighted), axis=0), cg2[hg[h], :length, :])
            send_s[span, :] = both[:HEADDIM] + both[HEADDIM:]

        @pl.when(is_last)
        def _():
            chain(k).start()

        return carry

    chunks = heads // CHUNK_HEADS
    lax.fori_loop(0, chunks, own_chunk, 0)

    both_t = jnp.concatenate([cum, timestep, jnp.zeros((length - 2 * heads, length), f32)], axis=0).T
    for h in range(heads):
        cumb[h] = jnp.broadcast_to(both_t[:, h:h + 1], (length, length))
        stepb[h] = jnp.broadcast_to(both_t[:, heads + h:heads + h + 1], (length, length))

    low_lanes = lax.broadcasted_iota(jnp.int32, (length, 128), 1) < HEADDIM
    ones = jnp.ones((8, 256), bf16)

    def main_chunk(k, carry):
        @pl.when(ctx < n_ctx - 1)
        def _():
            chain(k).wait_recv()

        @pl.when(jnp.logical_and(ctx < n_ctx - 1, ctx > 0))
        def _():
            for e in range(CHUNK_HEADS):
                h = k * CHUNK_HEADS + e
                span = pl.ds(pl.multiple_of(h * HEADDIM, HEADDIM), HEADDIM)
                send_s[span, :] = send_s[span, :] + elast_s[pl.ds(h, 1), :] * recv_s[span, :]
            chain(k).start()

        grads = []
        for q in range(CHUNK_HEADS // 2):
            pair = k * (CHUNK_HEADS // 2) + q
            lanes = pl.ds(pl.multiple_of(pair * 128, 128), 128)
            xp = x[:, lanes]
            cp = cot[:, lanes]
            incoming = recv_s[lanes, :]
            rhs = jnp.concatenate(split(incoming), axis=0)
            product_state = incoming * st[lanes, :].astype(f32)
            for e in range(2):
                h = pair * 2 + e
                g = hg[h]
                row = pl.ds(h, 1)
                span = pl.ds(pl.multiple_of(h * HEADDIM, HEADDIM), HEADDIM)
                mask = low_lanes if e == 0 else jnp.logical_not(low_lanes)
                xm = jnp.where(mask, xp, jnp.zeros_like(xp))
                c2 = cg2[g]
                cum_h = cumb[h]
                step_h = stepb[h]
                gaps = cum_s[row, :] - cum_h
                decay = jnp.where(causal, jnp.exp(jnp.where(causal, gaps, 0.0)), 0.0)
                m = decay * mm_nt(xm, cp)
                scored = m * sc[g]
                x_state = mm(jnp.concatenate([xm, xm], axis=1), rhs)
                to_end = jnp.exp(last_s[row, :] - cum_h)
                grads.append((h, step_h * (mm(jnp.concatenate(split(m), axis=1), c2) + to_end * x_state)))
                row_s[row, :] = jnp.sum(scored * step_h, axis=0, keepdims=True)
                col_s[row, :] = mm_nt(ones, jnp.concatenate(split(scored), axis=1))[:1]
                end_s[row, :] = mm_nt(ones, jnp.concatenate(split(x_state * bg[g]), axis=1))[:1]
                carried = mm_nt(st[span, :], c2[:length])
                car_s[row, :] = jnp.sum(cot_t[span, :].astype(f32) * carried, axis=0, keepdims=True)
                gs_s[row, :] = jnp.sum(
                    product_state[e * HEADDIM:(e + 1) * HEADDIM], axis=0, keepdims=True)
        for g in range(GROUPS):
            total = acc[g]
            for h, value in grads:
                total = total + jnp.where(hg[h] == g, 1.0, 0.0) * value
            acc[g] = total
        return carry

    fetches[4].wait()
    fetches[5].wait()
    lax.fori_loop(0, chunks, main_chunk, 0)

    col = col_s[...]
    end_plain = jnp.exp(last_s[...] - cum_s[...]) * end_s[...]
    end_term = end_plain * timestep
    grad_cum = row_s[...] - col * timestep + growth_s[...] * car_s[...] - end_term
    end_total = jnp.sum(end_term, axis=1, keepdims=True) + elast_s[:, :1] * jnp.sum(gs_s[...], axis=1, keepdims=True)
    lane = lax.broadcasted_iota(jnp.int32, (heads, length), 1)
    grad_cum = grad_cum + jnp.where(lane == length - 1, end_total, 0.0)
    backward = jnp.dot(grad_cum, (rows >= cols).astype(f32), precision=exact, preferred_element_type=f32)
    grad_raw = (col + end_plain - rate_c * backward) * gain

    def g_copy(r, peer, slot):
        return pltpu.make_async_remote_copy(
            src_ref=graw_own, dst_ref=graw_all.at[slot], send_sem=g_send.at[r], recv_sem=g_recv.at[r],
            device_id=(peer, ctx), device_id_type=MESH)

    def p_copy(r, peer, slot):
        return pltpu.make_async_remote_copy(
            src_ref=part, dst_ref=p_all.at[slot], send_sem=p_send.at[r], recv_sem=p_recv.at[r],
            device_id=(dp, peer), device_id_type=MESH)

    if fuse:
        graw_own[...] = grad_raw
        for r in range(1, n_dp):
            g_copy(r, lax.rem(dp + r, n_dp), dp).start()
        graw_all[dp] = grad_raw
    else:
        out_w[...] = grad_raw

    for g in range(GROUPS):
        out_b[:, pl.ds(NSTATE * g, NSTATE)] = acc[g].astype(bf16)

    if fuse:
        total = jnp.zeros((2 * heads, depth), f32)
        for r in range(1, n_dp):
            source = lax.rem(dp - r + n_dp, n_dp)
            h_copy(r, lax.rem(dp + r, n_dp), source).wait_recv()
        for r in range(1, n_dp):
            source = lax.rem(dp - r + n_dp, n_dp)
            g_copy(r, lax.rem(dp + r, n_dp), source).wait_recv()
        for d in range(n_dp):
            total = total + mm(jnp.concatenate(split(graw_all[d]), axis=0), hall[d])
        part[...] = total[:heads] + total[heads:]
        for r in range(1, n_ctx):
            p_copy(r, lax.rem(ctx + r, n_ctx), ctx).start()
        p_all[ctx] = part[...]
        for r in range(1, n_ctx):
            p_copy(r, lax.rem(ctx + r, n_ctx), lax.rem(ctx - r + n_ctx, n_ctx)).wait_recv()
        summed = p_all[0]
        for d in range(1, n_ctx):
            summed = summed + p_all[d]
        out_w[...] = summed
        for r in range(1, n_ctx):
            p_copy(r, lax.rem(ctx + r, n_ctx), ctx).wait_send()
        for r in range(1, n_dp):
            h_copy(r, lax.rem(dp + r, n_dp), dp).wait_send()
            g_copy(r, lax.rem(dp + r, n_dp), dp).wait_send()

    if gather:
        for r in range(1, n_dp):
            w_copy(r, lax.rem(dp + r, n_dp), dp).wait_send()

    @pl.when(ctx > 0)
    def _():
        def drain(k, carry):
            chain(k).wait_send()
            return carry

        lax.fori_loop(0, chunks, drain, 0)


def body(n_dp, n_ctx, hidden, dt_weight, ssm_input, grad_output, b_matrix, c_matrix,
         stored_states, step_bias, decay_code, head_group):
    length, width = hidden.shape[1:]
    depth = dt_weight.shape[0]
    heads = step_bias.shape[0]
    gather = depth % 128 == 0
    fuse = FUSE_END and gather
    hid = hidden[0]
    if gather:
        w = dt_weight.T
    else:
        w = lax.all_gather(dt_weight.T, "dp", axis=0, tiled=False)
    chunks = heads // CHUNK_HEADS
    any_ = pl.BlockSpec(memory_space=pl.ANY)
    vmem = pl.BlockSpec(memory_space=pltpu.VMEM)
    small = pltpu.VMEM((heads, length), f32)
    dma = pltpu.SemaphoreType.DMA
    scratch = [
        pltpu.VMEM((n_dp if gather else 1, heads, depth), bf16),
        pltpu.VMEM((heads * HEADDIM, length), bf16),
        pltpu.VMEM((GROUPS, length, NSTATE), f32),
        pltpu.VMEM((GROUPS, 2 * length, NSTATE), bf16),
        pltpu.VMEM((GROUPS, length, length), f32),
        small, small, small, small,
        pltpu.VMEM((heads, length, length), f32),
        pltpu.VMEM((heads, length, length), f32),
        pltpu.VMEM((GROUPS, length, NSTATE), f32),
        small, small, small, small, small,
        pltpu.VMEM((heads * HEADDIM, NSTATE), f32),
        pltpu.VMEM((heads * HEADDIM, NSTATE), f32),
        pltpu.VMEM(hid.shape, bf16),
        pltpu.VMEM(ssm_input.shape[1:], bf16),
        pltpu.VMEM(grad_output.shape[1:], bf16),
        pltpu.VMEM(b_matrix.shape[1:], bf16),
        pltpu.VMEM(c_matrix.shape[1:], bf16),
        pltpu.VMEM((heads * HEADDIM, NSTATE), bf16),
        dma((7,)),
        dma((n_dp,)), dma((n_dp,)), dma((chunks,)), dma((chunks,)),
    ]
    if fuse:
        scratch += [
            pltpu.VMEM((n_dp, length, depth), bf16),
            small,
            pltpu.VMEM((n_dp, heads, length), f32),
            pltpu.VMEM((heads, depth), f32),
            dma((n_dp,)), dma((n_dp,)), dma((n_dp,)), dma((n_dp,)),
            pltpu.VMEM((n_ctx, heads, depth), f32),
            dma((n_ctx,)), dma((n_ctx,)),
        ]
    grad_b, res = pl.pallas_call(
        functools.partial(kernel, (n_dp, n_ctx, gather, fuse)),
        out_shape=(
            jax.ShapeDtypeStruct((length, GROUPS * NSTATE), bf16),
            jax.ShapeDtypeStruct((heads, depth if fuse else length), f32),
        ),
        in_specs=[any_] + [any_ if gather else vmem] + [any_] * 5 + [vmem] * 2 + [pl.BlockSpec(memory_space=pltpu.SMEM)],
        out_specs=(vmem, vmem),
        scratch_shapes=scratch,
        compiler_params=pltpu.CompilerParams(
            collective_id=0, has_side_effects=True, vmem_limit_bytes=48 * 1024 * 1024),
    )(hid, w, ssm_input[0], grad_output[0], b_matrix[0], c_matrix[0],
      stored_states.reshape(heads * HEADDIM, NSTATE), step_bias.reshape(1, heads),
      decay_code.reshape(1, heads), head_group)
    if fuse:
        grad_w = res.T
    else:
        hi = lax.reduce_precision(res, 8, 7)
        both = mm(jnp.concatenate([hi.astype(bf16), (res - hi).astype(bf16)], axis=0), hid)
        part = both[:heads] + both[heads:]
        part = lax.psum_scatter(part, "dp", scatter_dimension=1, tiled=True)
        grad_w = lax.psum(part, "ctx").T
    return grad_b[None], grad_w


def solution(mesh):
    return jax.shard_map(
        functools.partial(body, mesh.shape["dp"], mesh.shape["ctx"]),
        mesh=mesh,
        in_specs=(
            P("dp", "ctx", None),
            P("dp", None),
            P("dp", "ctx", None),
            P("dp", "ctx", None),
            P("dp", "ctx", None),
            P("dp", "ctx", None),
            P("dp", "ctx", None, None, None),
            P(),
            P(),
            P(),
        ),
        out_specs=(P("dp", "ctx", None), P("dp", None)),
        check_vma=False,
    )
```

```python
import functools

import jax
import jax.numpy as jnp
from jax import lax
from jax.experimental import pallas as pl
from jax.experimental.pallas import tpu as pltpu
from jax.sharding import PartitionSpec as P

HEADDIM = 64
NSTATE = 128
GROUPS = 8
CHUNK_HEADS = 2
FUSE_END = True

f32, bf16 = jnp.float32, jnp.bfloat16
MESH = pl.DeviceIdType.MESH
exact = lax.Precision.HIGHEST


def mm(a, b):
    return jnp.dot(a, b, preferred_element_type=f32)


def mm_nt(a, b):
    return lax.dot_general(a, b, (((1,), (1,)), ((), ())), preferred_element_type=f32)


def split(v):
    hi = v.astype(bf16)
    return hi, (v - hi.astype(f32)).astype(bf16)


def kernel(cfg, hid_h, w, x_h, cot_h, b_h, c_h, st_h, bias, code, hg, *rest):
    n_dp, n_ctx, gather, fuse = cfg
    (out_b, out_w), rest = rest[:2], rest[2:]
    (wall, cot_t, bg, cg2, sc, cum_s, last_s, growth_s, elast_s, cumb, stepb, acc,
     row_s, col_s, car_s, end_s, gs_s, send_s, recv_s, hid, x, cot, b, c, st, in_sem,
     w_send, w_recv, ch_send, ch_recv) = rest[:30]
    length = x.shape[0]
    heads = bias.shape[1]
    depth = hid.shape[1] // n_dp
    full_length = length * n_ctx
    dp = lax.axis_index("dp")
    ctx = lax.axis_index("ctx")
    is_last = ctx == n_ctx - 1

    if fuse:
        hall, graw_own, graw_all, part, h_send, h_recv, g_send, g_recv, p_all, p_send, p_recv = rest[30:]

    fetches = [
        pltpu.make_async_copy(source, target, in_sem.at[i])
        for i, (source, target) in enumerate(
            ((cot_h, cot), (c_h, c), (b_h, b), (hid_h, hid), (x_h, x), (st_h, st)))
    ]
    own_w = pltpu.make_async_copy(w, wall.at[dp if gather else 0], in_sem.at[6])
    barrier = pltpu.get_barrier_semaphore()
    if gather or fuse:
        for r in range(1, n_dp):
            pl.semaphore_signal(barrier, inc=1, device_id=(lax.rem(dp + r, n_dp), ctx), device_id_type=MESH)
    for r in range(1, n_ctx):
        pl.semaphore_signal(barrier, inc=1, device_id=(dp, lax.rem(ctx + r, n_ctx)), device_id_type=MESH)

    ri = lax.broadcasted_iota(jnp.int32, (heads, heads), 0)
    ci = lax.broadcasted_iota(jnp.int32, (heads, heads), 1)
    eye = ri == ci
    if gather:
        own_w.start()
    for fetch in fetches:
        fetch.start()
    pl.semaphore_wait(barrier, (n_dp - 1 if gather or fuse else 0) + n_ctx - 1)

    def w_copy(r, peer, slot):
        return pltpu.make_async_remote_copy(
            src_ref=w, dst_ref=wall.at[slot], send_sem=w_send.at[r], recv_sem=w_recv.at[r],
            device_id=(peer, ctx), device_id_type=MESH)

    def h_copy(r, peer, slot):
        return pltpu.make_async_remote_copy(
            src_ref=hid_h.at[:, pl.ds(pl.multiple_of(peer * depth, depth), depth)], dst_ref=hall.at[slot],
            send_sem=h_send.at[r], recv_sem=h_recv.at[r], device_id=(peer, ctx), device_id_type=MESH)

    if gather:
        for r in range(1, n_dp):
            w_copy(r, lax.rem(dp + r, n_dp), dp).start()
    if fuse:
        for r in range(1, n_dp):
            h_copy(r, lax.rem(dp + r, n_dp), dp).start()

    fetches[0].wait()
    for k in range(x.shape[1] // 128):
        cot_t[pl.ds(128 * k, 128), :] = cot[:, pl.ds(128 * k, 128)].T
    fetches[1].wait()
    fetches[2].wait()
    for g in range(GROUPS):
        b_g = b[:, pl.ds(NSTATE * g, NSTATE)]
        c_g = c[:, pl.ds(NSTATE * g, NSTATE)]
        bg[g] = b_g.astype(f32)
        cg2[g, :length, :] = c_g
        cg2[g, length:, :] = c_g
        sc[g] = mm_nt(b_g, c_g)
    acc[...] = jnp.zeros_like(acc)

    @pl.when(is_last)
    def _():
        recv_s[...] = jnp.zeros_like(recv_s)

    bias_c = jnp.sum(jnp.where(eye, bias[...], 0.0), axis=1, keepdims=True)
    rate_c = jnp.sum(jnp.where(eye, code[...].astype(f32), 0.0), axis=1, keepdims=True) / (256.0 * full_length)

    fetches[3].wait()
    if fuse:
        hall[dp] = hid[:, pl.ds(pl.multiple_of(dp * depth, depth), depth)]
    if gather:
        own_w.wait()
        for r in range(1, n_dp):
            w_copy(r, lax.rem(dp + r, n_dp), lax.rem(dp - r + n_dp, n_dp)).wait_recv()
    proj = jnp.zeros((heads, length), f32)
    for d in range(n_dp):
        proj = proj + mm_nt(wall[d] if gather else w[d], hid[:, d * depth:(d + 1) * depth])
    shifted = proj + bias_c
    timestep = jnp.maximum(shifted, 0.0) + jnp.log1p(jnp.exp(-jnp.abs(shifted)))
    gain = 1.0 / (1.0 + jnp.exp(-shifted))
    rows = lax.broadcasted_iota(jnp.int32, (length, length), 0)
    cols = lax.broadcasted_iota(jnp.int32, (length, length), 1)
    causal = rows <= cols
    cum = jnp.dot(-rate_c * timestep, causal.astype(f32), precision=exact, preferred_element_type=f32)
    last = jnp.broadcast_to(cum[:, length - 1:length], (heads, length))
    cum_s[...] = cum
    last_s[...] = last
    growth_s[...] = jnp.exp(cum)
    elast_s[...] = jnp.exp(last)

    def chain(k):
        span = pl.ds(pl.multiple_of(k * (CHUNK_HEADS * HEADDIM), CHUNK_HEADS * HEADDIM), CHUNK_HEADS * HEADDIM)
        return pltpu.make_async_remote_copy(
            src_ref=send_s.at[span], dst_ref=recv_s.at[span], send_sem=ch_send.at[k], recv_sem=ch_recv.at[k],
            device_id=(dp, lax.rem(ctx - 1 + n_ctx, n_ctx)), device_id_type=MESH)

    def own_chunk(k, carry):
        for e in range(CHUNK_HEADS):
            h = k * CHUNK_HEADS + e
            span = pl.ds(pl.multiple_of(h * HEADDIM, HEADDIM), HEADDIM)
            weighted = cot_t[span, :].astype(f32) * growth_s[pl.ds(h, 1), :]
            both = mm(jnp.concatenate(split(weighted), axis=0), cg2[hg[h], :length, :])
            send_s[span, :] = both[:HEADDIM] + both[HEADDIM:]

        @pl.when(is_last)
        def _():
            chain(k).start()

        return carry

    chunks = heads // CHUNK_HEADS
    lax.fori_loop(0, chunks, own_chunk, 0)

    both_t = jnp.concatenate([cum, timestep, jnp.zeros((length - 2 * heads, length), f32)], axis=0).T
    for h in range(heads):
        cumb[h] = jnp.broadcast_to(both_t[:, h:h + 1], (length, length))
        stepb[h] = jnp.broadcast_to(both_t[:, heads + h:heads + h + 1], (length, length))

    low_lanes = lax.broadcasted_iota(jnp.int32, (length, 128), 1) < HEADDIM
    ones = jnp.ones((8, 256), bf16)

    def main_chunk(k, carry):
        @pl.when(ctx < n_ctx - 1)
        def _():
            chain(k).wait_recv()

        @pl.when(jnp.logical_and(ctx < n_ctx - 1, ctx > 0))
        def _():
            for e in range(CHUNK_HEADS):
                h = k * CHUNK_HEADS + e
                span = pl.ds(pl.multiple_of(h * HEADDIM, HEADDIM), HEADDIM)
                send_s[span, :] = send_s[span, :] + elast_s[pl.ds(h, 1), :] * recv_s[span, :]
            chain(k).start()

        grads = []
        for q in range(CHUNK_HEADS // 2):
            pair = k * (CHUNK_HEADS // 2) + q
            lanes = pl.ds(pl.multiple_of(pair * 128, 128), 128)
            xp = x[:, lanes]
            cp = cot[:, lanes]
            incoming = recv_s[lanes, :]
            rhs = jnp.concatenate(split(incoming), axis=0)
            product_state = incoming * st[lanes, :].astype(f32)
            for e in range(2):
                h = pair * 2 + e
                g = hg[h]
                row = pl.ds(h, 1)
                span = pl.ds(pl.multiple_of(h * HEADDIM, HEADDIM), HEADDIM)
                mask = low_lanes if e == 0 else jnp.logical_not(low_lanes)
                xm = jnp.where(mask, xp, jnp.zeros_like(xp))
                c2 = cg2[g]
                cum_h = cumb[h]
                step_h = stepb[h]
                gaps = cum_s[row, :] - cum_h
                decay = jnp.where(causal, jnp.exp(jnp.where(causal, gaps, 0.0)), 0.0)
                m = decay * mm_nt(xm, cp)
                scored = m * sc[g]
                x_state = mm(jnp.concatenate([xm, xm], axis=1), rhs)
                to_end = jnp.exp(last_s[row, :] - cum_h)
                grads.append((h, step_h * (mm(jnp.concatenate(split(m), axis=1), c2) + to_end * x_state)))
                row_s[row, :] = jnp.sum(scored * step_h, axis=0, keepdims=True)
                col_s[row, :] = mm_nt(ones, jnp.concatenate(split(scored), axis=1))[:1]
                end_s[row, :] = mm_nt(ones, jnp.concatenate(split(x_state * bg[g]), axis=1))[:1]
                carried = mm_nt(st[span, :], c2[:length])
                car_s[row, :] = jnp.sum(cot_t[span, :].astype(f32) * carried, axis=0, keepdims=True)
                gs_s[row, :] = jnp.sum(
                    product_state[e * HEADDIM:(e + 1) * HEADDIM], axis=0, keepdims=True)
        for g in range(GROUPS):
            total = acc[g]
            for h, value in grads:
                total = total + jnp.where(hg[h] == g, 1.0, 0.0) * value
            acc[g] = total
        return carry

    fetches[4].wait()
    fetches[5].wait()
    lax.fori_loop(0, chunks, main_chunk, 0)

    col = col_s[...]
    end_plain = jnp.exp(last_s[...] - cum_s[...]) * end_s[...]
    end_term = end_plain * timestep
    grad_cum = row_s[...] - col * timestep + growth_s[...] * car_s[...] - end_term
    end_total = jnp.sum(end_term, axis=1, keepdims=True) + elast_s[:, :1] * jnp.sum(gs_s[...], axis=1, keepdims=True)
    lane = lax.broadcasted_iota(jnp.int32, (heads, length), 1)
    grad_cum = grad_cum + jnp.where(lane == length - 1, end_total, 0.0)
    backward = jnp.dot(grad_cum, (rows >= cols).astype(f32), precision=exact, preferred_element_type=f32)
    grad_raw = (col + end_plain - rate_c * backward) * gain

    def g_copy(r, peer, slot):
        return pltpu.make_async_remote_copy(
            src_ref=graw_own, dst_ref=graw_all.at[slot], send_sem=g_send.at[r], recv_sem=g_recv.at[r],
            device_id=(peer, ctx), device_id_type=MESH)

    def p_copy(r, peer, slot):
        return pltpu.make_async_remote_copy(
            src_ref=part, dst_ref=p_all.at[slot], send_sem=p_send.at[r], recv_sem=p_recv.at[r],
            device_id=(dp, peer), device_id_type=MESH)

    if fuse:
        graw_own[...] = grad_raw
        for r in range(1, n_dp):
            g_copy(r, lax.rem(dp + r, n_dp), dp).start()
        graw_all[dp] = grad_raw
    else:
        out_w[...] = grad_raw

    for g in range(GROUPS):
        out_b[:, pl.ds(NSTATE * g, NSTATE)] = acc[g].astype(bf16)

    if fuse:
        total = jnp.zeros((2 * heads, depth), f32)
        for r in range(1, n_dp):
            source = lax.rem(dp - r + n_dp, n_dp)
            h_copy(r, lax.rem(dp + r, n_dp), source).wait_recv()
        for r in range(1, n_dp):
            source = lax.rem(dp - r + n_dp, n_dp)
            g_copy(r, lax.rem(dp + r, n_dp), source).wait_recv()
        for d in range(n_dp):
            total = total + mm(jnp.concatenate(split(graw_all[d]), axis=0), hall[d])
        part[...] = total[:heads] + total[heads:]
        for r in range(1, n_ctx):
            p_copy(r, lax.rem(ctx + r, n_ctx), ctx).start()
        p_all[ctx] = part[...]
        for r in range(1, n_ctx):
            p_copy(r, lax.rem(ctx + r, n_ctx), lax.rem(ctx - r + n_ctx, n_ctx)).wait_recv()
        summed = p_all[0]
        for d in range(1, n_ctx):
            summed = summed + p_all[d]
        out_w[...] = summed
        for r in range(1, n_ctx):
            p_copy(r, lax.rem(ctx + r, n_ctx), ctx).wait_send()
        for r in range(1, n_dp):
            h_copy(r, lax.rem(dp + r, n_dp), dp).wait_send()
            g_copy(r, lax.rem(dp + r, n_dp), dp).wait_send()

    if gather:
        for r in range(1, n_dp):
            w_copy(r, lax.rem(dp + r, n_dp), dp).wait_send()

    @pl.when(ctx > 0)
    def _():
        def drain(k, carry):
            chain(k).wait_send()
            return carry

        lax.fori_loop(0, chunks, drain, 0)


def body(n_dp, n_ctx, hidden, dt_weight, ssm_input, grad_output, b_matrix, c_matrix,
         stored_states, step_bias, decay_code, head_group):
    length, width = hidden.shape[1:]
    depth = dt_weight.shape[0]
    heads = step_bias.shape[0]
    gather = depth % 128 == 0
    fuse = FUSE_END and gather
    hid = hidden[0]
    if gather:
        w = dt_weight.T
    else:
        w = lax.all_gather(dt_weight.T, "dp", axis=0, tiled=False)
    chunks = heads // CHUNK_HEADS
    any_ = pl.BlockSpec(memory_space=pltpu.HBM)
    vmem = pl.BlockSpec(memory_space=pltpu.VMEM)
    small = pltpu.VMEM((heads, length), f32)
    dma = pltpu.SemaphoreType.DMA
    scratch = [
        pltpu.VMEM((n_dp if gather else 1, heads, depth), bf16),
        pltpu.VMEM((heads * HEADDIM, length), bf16),
        pltpu.VMEM((GROUPS, length, NSTATE), f32),
        pltpu.VMEM((GROUPS, 2 * length, NSTATE), bf16),
        pltpu.VMEM((GROUPS, length, length), f32),
        small, small, small, small,
        pltpu.VMEM((heads, length, length), f32),
        pltpu.VMEM((heads, length, length), f32),
        pltpu.VMEM((GROUPS, length, NSTATE), f32),
        small, small, small, small, small,
        pltpu.VMEM((heads * HEADDIM, NSTATE), f32),
        pltpu.VMEM((heads * HEADDIM, NSTATE), f32),
        pltpu.VMEM(hid.shape, bf16),
        pltpu.VMEM(ssm_input.shape[1:], bf16),
        pltpu.VMEM(grad_output.shape[1:], bf16),
        pltpu.VMEM(b_matrix.shape[1:], bf16),
        pltpu.VMEM(c_matrix.shape[1:], bf16),
        pltpu.VMEM((heads * HEADDIM, NSTATE), bf16),
        dma((7,)),
        dma((n_dp,)), dma((n_dp,)), dma((chunks,)), dma((chunks,)),
    ]
    if fuse:
        scratch += [
            pltpu.VMEM((n_dp, length, depth), bf16),
            small,
            pltpu.VMEM((n_dp, heads, length), f32),
            pltpu.VMEM((heads, depth), f32),
            dma((n_dp,)), dma((n_dp,)), dma((n_dp,)), dma((n_dp,)),
            pltpu.VMEM((n_ctx, heads, depth), f32),
            dma((n_ctx,)), dma((n_ctx,)),
        ]
    grad_b, res = pl.pallas_call(
        functools.partial(kernel, (n_dp, n_ctx, gather, fuse)),
        out_shape=(
            jax.ShapeDtypeStruct((length, GROUPS * NSTATE), bf16),
            jax.ShapeDtypeStruct((heads, depth if fuse else length), f32),
        ),
        in_specs=[any_] + [any_ if gather else vmem] + [any_] * 5 + [vmem] * 2 + [pl.BlockSpec(memory_space=pltpu.SMEM)],
        out_specs=(vmem, vmem),
        scratch_shapes=scratch,
        compiler_params=pltpu.CompilerParams(
            collective_id=0, has_side_effects=True, vmem_limit_bytes=48 * 1024 * 1024),
    )(hid, w, ssm_input[0], grad_output[0], b_matrix[0], c_matrix[0],
      stored_states.reshape(heads * HEADDIM, NSTATE), step_bias.reshape(1, heads),
      decay_code.reshape(1, heads), head_group)
    if fuse:
        grad_w = res.T
    else:
        hi = lax.reduce_precision(res, 8, 7)
        both = mm(jnp.concatenate([hi.astype(bf16), (res - hi).astype(bf16)], axis=0), hid)
        part = both[:heads] + both[heads:]
        part = lax.psum_scatter(part, "dp", scatter_dimension=1, tiled=True)
        grad_w = lax.psum(part, "ctx").T
    return grad_b[None], grad_w


def solution(mesh):
    return jax.shard_map(
        functools.partial(body, mesh.shape["dp"], mesh.shape["ctx"]),
        mesh=mesh,
        in_specs=(
            P("dp", "ctx", None),
            P("dp", None),
            P("dp", "ctx", None),
            P("dp", "ctx", None),
            P("dp", "ctx", None),
            P("dp", "ctx", None),
            P("dp", "ctx", None, None, None),
            P(),
            P(),
            P(),
        ),
        out_specs=(P("dp", "ctx", None), P("dp", None)),
        check_vma=False,
    )
```

```python
import functools

import jax
import jax.numpy as jnp
from jax import lax
from jax.experimental import pallas as pl
from jax.experimental.pallas import tpu as pltpu
from jax.sharding import PartitionSpec as P

HEADDIM = 64
NSTATE = 128
GROUPS = 8
CHUNK_HEADS = 2
FUSE_END = True

f32, bf16 = jnp.float32, jnp.bfloat16
MESH = pl.DeviceIdType.MESH
exact = lax.Precision.HIGHEST


def mm(a, b):
    return jnp.dot(a, b, preferred_element_type=f32)


def mm_nt(a, b):
    return lax.dot_general(a, b, (((1,), (1,)), ((), ())), preferred_element_type=f32)


def split(v):
    hi = v.astype(bf16)
    return hi, (v - hi.astype(f32)).astype(bf16)


def kernel(cfg, hid_h, w, x_h, cot_h, b_h, c_h, st_h, bias, code, hg, *rest):
    n_dp, n_ctx, gather, fuse = cfg
    (out_b, out_w), rest = rest[:2], rest[2:]
    (wall, cot_t, bg, cg2, sc, cum_s, last_s, growth_s, elast_s, cumb, stepb, acc,
     row_s, col_s, car_s, end_s, gs_s, send_s, recv_s, hid, x, cot, b, c, st, in_sem,
     w_send, w_recv, ch_send, ch_recv) = rest[:30]
    length = x.shape[0]
    heads = bias.shape[1]
    depth = hid.shape[1] // n_dp
    full_length = length * n_ctx
    dp = lax.axis_index("dp")
    ctx = lax.axis_index("ctx")
    is_last = ctx == n_ctx - 1

    if fuse:
        hall, graw_own, graw_all, part, h_send, h_recv, g_send, g_recv, p_all, p_send, p_recv, mine, final, q_send, q_recv = rest[30:]

    fetches = [
        pltpu.make_async_copy(source, target, in_sem.at[i])
        for i, (source, target) in enumerate(
            ((cot_h, cot), (c_h, c), (b_h, b), (hid_h, hid), (x_h, x), (st_h, st)))
    ]
    own_w = pltpu.make_async_copy(w, wall.at[dp if gather else 0], in_sem.at[6])
    barrier = pltpu.get_barrier_semaphore()
    if gather or fuse:
        for r in range(1, n_dp):
            pl.semaphore_signal(barrier, inc=1, device_id=(lax.rem(dp + r, n_dp), ctx), device_id_type=MESH)
    for r in range(1, n_ctx):
        pl.semaphore_signal(barrier, inc=1, device_id=(dp, lax.rem(ctx + r, n_ctx)), device_id_type=MESH)

    ri = lax.broadcasted_iota(jnp.int32, (heads, heads), 0)
    ci = lax.broadcasted_iota(jnp.int32, (heads, heads), 1)
    eye = ri == ci
    if gather:
        own_w.start()
    for fetch in fetches:
        fetch.start()
    pl.semaphore_wait(barrier, (n_dp - 1 if gather or fuse else 0) + n_ctx - 1)

    def w_copy(r, peer, slot):
        return pltpu.make_async_remote_copy(
            src_ref=w, dst_ref=wall.at[slot], send_sem=w_send.at[r], recv_sem=w_recv.at[r],
            device_id=(peer, ctx), device_id_type=MESH)

    def h_copy(r, peer, slot):
        return pltpu.make_async_remote_copy(
            src_ref=hid_h.at[:, pl.ds(pl.multiple_of(peer * depth, depth), depth)], dst_ref=hall.at[slot],
            send_sem=h_send.at[r], recv_sem=h_recv.at[r], device_id=(peer, ctx), device_id_type=MESH)

    if gather:
        for r in range(1, n_dp):
            w_copy(r, lax.rem(dp + r, n_dp), dp).start()
    if fuse:
        for r in range(1, n_dp):
            h_copy(r, lax.rem(dp + r, n_dp), dp).start()

    fetches[0].wait()
    for k in range(x.shape[1] // 128):
        cot_t[pl.ds(128 * k, 128), :] = cot[:, pl.ds(128 * k, 128)].T
    fetches[1].wait()
    fetches[2].wait()
    for g in range(GROUPS):
        b_g = b[:, pl.ds(NSTATE * g, NSTATE)]
        c_g = c[:, pl.ds(NSTATE * g, NSTATE)]
        bg[g] = b_g.astype(f32)
        cg2[g, :length, :] = c_g
        cg2[g, length:, :] = c_g
        sc[g] = mm_nt(b_g, c_g)
    acc[...] = jnp.zeros_like(acc)

    @pl.when(is_last)
    def _():
        recv_s[...] = jnp.zeros_like(recv_s)

    bias_c = jnp.sum(jnp.where(eye, bias[...], 0.0), axis=1, keepdims=True)
    rate_c = jnp.sum(jnp.where(eye, code[...].astype(f32), 0.0), axis=1, keepdims=True) / (256.0 * full_length)

    fetches[3].wait()
    if fuse:
        hall[dp] = hid[:, pl.ds(pl.multiple_of(dp * depth, depth), depth)]
    if gather:
        own_w.wait()
        for r in range(1, n_dp):
            w_copy(r, lax.rem(dp + r, n_dp), lax.rem(dp - r + n_dp, n_dp)).wait_recv()
    proj = jnp.zeros((heads, length), f32)
    for d in range(n_dp):
        proj = proj + mm_nt(wall[d] if gather else w[d], hid[:, d * depth:(d + 1) * depth])
    shifted = proj + bias_c
    timestep = jnp.maximum(shifted, 0.0) + jnp.log1p(jnp.exp(-jnp.abs(shifted)))
    gain = 1.0 / (1.0 + jnp.exp(-shifted))
    rows = lax.broadcasted_iota(jnp.int32, (length, length), 0)
    cols = lax.broadcasted_iota(jnp.int32, (length, length), 1)
    causal = rows <= cols
    cum = jnp.dot(-rate_c * timestep, causal.astype(f32), precision=exact, preferred_element_type=f32)
    last = jnp.broadcast_to(cum[:, length - 1:length], (heads, length))
    cum_s[...] = cum
    last_s[...] = last
    growth_s[...] = jnp.exp(cum)
    elast_s[...] = jnp.exp(last)

    def chain(k):
        span = pl.ds(pl.multiple_of(k * (CHUNK_HEADS * HEADDIM), CHUNK_HEADS * HEADDIM), CHUNK_HEADS * HEADDIM)
        return pltpu.make_async_remote_copy(
            src_ref=send_s.at[span], dst_ref=recv_s.at[span], send_sem=ch_send.at[k], recv_sem=ch_recv.at[k],
            device_id=(dp, lax.rem(ctx - 1 + n_ctx, n_ctx)), device_id_type=MESH)

    def own_chunk(k, carry):
        for e in range(CHUNK_HEADS):
            h = k * CHUNK_HEADS + e
            span = pl.ds(pl.multiple_of(h * HEADDIM, HEADDIM), HEADDIM)
            weighted = cot_t[span, :].astype(f32) * growth_s[pl.ds(h, 1), :]
            both = mm(jnp.concatenate(split(weighted), axis=0), cg2[hg[h], :length, :])
            send_s[span, :] = both[:HEADDIM] + both[HEADDIM:]

        @pl.when(is_last)
        def _():
            chain(k).start()

        return carry

    chunks = heads // CHUNK_HEADS
    lax.fori_loop(0, chunks, own_chunk, 0)

    both_t = jnp.concatenate([cum, timestep, jnp.zeros((length - 2 * heads, length), f32)], axis=0).T
    for h in range(heads):
        cumb[h] = jnp.broadcast_to(both_t[:, h:h + 1], (length, length))
        stepb[h] = jnp.broadcast_to(both_t[:, heads + h:heads + h + 1], (length, length))

    low_lanes = lax.broadcasted_iota(jnp.int32, (length, 128), 1) < HEADDIM
    ones = jnp.ones((8, 256), bf16)

    def main_chunk(k, carry):
        @pl.when(ctx < n_ctx - 1)
        def _():
            chain(k).wait_recv()

        @pl.when(jnp.logical_and(ctx < n_ctx - 1, ctx > 0))
        def _():
            for e in range(CHUNK_HEADS):
                h = k * CHUNK_HEADS + e
                span = pl.ds(pl.multiple_of(h * HEADDIM, HEADDIM), HEADDIM)
                send_s[span, :] = send_s[span, :] + elast_s[pl.ds(h, 1), :] * recv_s[span, :]
            chain(k).start()

        grads = []
        for q in range(CHUNK_HEADS // 2):
            pair = k * (CHUNK_HEADS // 2) + q
            lanes = pl.ds(pl.multiple_of(pair * 128, 128), 128)
            xp = x[:, lanes]
            cp = cot[:, lanes]
            incoming = recv_s[lanes, :]
            rhs = jnp.concatenate(split(incoming), axis=0)
            product_state = incoming * st[lanes, :].astype(f32)
            for e in range(2):
                h = pair * 2 + e
                g = hg[h]
                row = pl.ds(h, 1)
                span = pl.ds(pl.multiple_of(h * HEADDIM, HEADDIM), HEADDIM)
                mask = low_lanes if e == 0 else jnp.logical_not(low_lanes)
                xm = jnp.where(mask, xp, jnp.zeros_like(xp))
                c2 = cg2[g]
                cum_h = cumb[h]
                step_h = stepb[h]
                gaps = cum_s[row, :] - cum_h
                decay = jnp.where(causal, jnp.exp(jnp.where(causal, gaps, 0.0)), 0.0)
                m = decay * mm_nt(xm, cp)
                scored = m * sc[g]
                x_state = mm(jnp.concatenate([xm, xm], axis=1), rhs)
                to_end = jnp.exp(last_s[row, :] - cum_h)
                grads.append((h, step_h * (mm(jnp.concatenate(split(m), axis=1), c2) + to_end * x_state)))
                row_s[row, :] = jnp.sum(scored * step_h, axis=0, keepdims=True)
                col_s[row, :] = mm_nt(ones, jnp.concatenate(split(scored), axis=1))[:1]
                end_s[row, :] = mm_nt(ones, jnp.concatenate(split(x_state * bg[g]), axis=1))[:1]
                carried = mm_nt(st[span, :], c2[:length])
                car_s[row, :] = jnp.sum(cot_t[span, :].astype(f32) * carried, axis=0, keepdims=True)
                gs_s[row, :] = jnp.sum(
                    product_state[e * HEADDIM:(e + 1) * HEADDIM], axis=0, keepdims=True)
        for g in range(GROUPS):
            total = acc[g]
            for h, value in grads:
                total = total + jnp.where(hg[h] == g, 1.0, 0.0) * value
            acc[g] = total
        return carry

    fetches[4].wait()
    fetches[5].wait()
    lax.fori_loop(0, chunks, main_chunk, 0)

    col = col_s[...]
    end_plain = jnp.exp(last_s[...] - cum_s[...]) * end_s[...]
    end_term = end_plain * timestep
    grad_cum = row_s[...] - col * timestep + growth_s[...] * car_s[...] - end_term
    end_total = jnp.sum(end_term, axis=1, keepdims=True) + elast_s[:, :1] * jnp.sum(gs_s[...], axis=1, keepdims=True)
    lane = lax.broadcasted_iota(jnp.int32, (heads, length), 1)
    grad_cum = grad_cum + jnp.where(lane == length - 1, end_total, 0.0)
    backward = jnp.dot(grad_cum, (rows >= cols).astype(f32), precision=exact, preferred_element_type=f32)
    grad_raw = (col + end_plain - rate_c * backward) * gain

    def g_copy(r, peer, slot):
        return pltpu.make_async_remote_copy(
            src_ref=graw_own, dst_ref=graw_all.at[slot], send_sem=g_send.at[r], recv_sem=g_recv.at[r],
            device_id=(peer, ctx), device_id_type=MESH)

    def p_copy(r, peer, slot):
        return pltpu.make_async_remote_copy(
            src_ref=part.at[peer], dst_ref=p_all.at[slot], send_sem=p_send.at[r], recv_sem=p_recv.at[r],
            device_id=(dp, peer), device_id_type=MESH)

    def q_copy(r, peer, slot):
        return pltpu.make_async_remote_copy(
            src_ref=mine, dst_ref=final.at[slot], send_sem=q_send.at[r], recv_sem=q_recv.at[r],
            device_id=(dp, peer), device_id_type=MESH)

    if fuse:
        graw_own[...] = grad_raw
        for r in range(1, n_dp):
            g_copy(r, lax.rem(dp + r, n_dp), dp).start()
        graw_all[dp] = grad_raw
    else:
        out_w[...] = grad_raw

    for g in range(GROUPS):
        out_b[:, pl.ds(NSTATE * g, NSTATE)] = acc[g].astype(bf16)

    if fuse:
        total = jnp.zeros((2 * heads, depth), f32)
        for r in range(1, n_dp):
            source = lax.rem(dp - r + n_dp, n_dp)
            h_copy(r, lax.rem(dp + r, n_dp), source).wait_recv()
        for r in range(1, n_dp):
            source = lax.rem(dp - r + n_dp, n_dp)
            g_copy(r, lax.rem(dp + r, n_dp), source).wait_recv()
        for d in range(n_dp):
            total = total + mm(jnp.concatenate(split(graw_all[d]), axis=0), hall[d])
        total = total[:heads] + total[heads:]
        piece = depth // n_ctx
        for d in range(n_ctx):
            part[d] = total[:, d * piece:(d + 1) * piece]
        for r in range(1, n_ctx):
            p_copy(r, lax.rem(ctx + r, n_ctx), ctx).start()
        p_all[ctx] = part[ctx]
        for r in range(1, n_ctx):
            p_copy(r, lax.rem(ctx + r, n_ctx), lax.rem(ctx - r + n_ctx, n_ctx)).wait_recv()
        summed = p_all[0]
        for d in range(1, n_ctx):
            summed = summed + p_all[d]
        mine[...] = summed
        for r in range(1, n_ctx):
            q_copy(r, lax.rem(ctx + r, n_ctx), ctx).start()
        final[ctx] = summed
        for r in range(1, n_ctx):
            q_copy(r, lax.rem(ctx + r, n_ctx), lax.rem(ctx - r + n_ctx, n_ctx)).wait_recv()
        for d in range(n_ctx):
            out_w[:, d * piece:(d + 1) * piece] = final[d]
        for r in range(1, n_ctx):
            p_copy(r, lax.rem(ctx + r, n_ctx), ctx).wait_send()
            q_copy(r, lax.rem(ctx + r, n_ctx), ctx).wait_send()
        for r in range(1, n_dp):
            h_copy(r, lax.rem(dp + r, n_dp), dp).wait_send()
            g_copy(r, lax.rem(dp + r, n_dp), dp).wait_send()

    if gather:
        for r in range(1, n_dp):
            w_copy(r, lax.rem(dp + r, n_dp), dp).wait_send()

    @pl.when(ctx > 0)
    def _():
        def drain(k, carry):
            chain(k).wait_send()
            return carry

        lax.fori_loop(0, chunks, drain, 0)


def body(n_dp, n_ctx, hidden, dt_weight, ssm_input, grad_output, b_matrix, c_matrix,
         stored_states, step_bias, decay_code, head_group):
    length, width = hidden.shape[1:]
    depth = dt_weight.shape[0]
    heads = step_bias.shape[0]
    gather = depth % 128 == 0
    fuse = FUSE_END and depth % (128 * n_ctx) == 0
    hid = hidden[0]
    if gather:
        w = dt_weight.T
    else:
        w = lax.all_gather(dt_weight.T, "dp", axis=0, tiled=False)
    chunks = heads // CHUNK_HEADS
    any_ = pl.BlockSpec(memory_space=pltpu.HBM)
    vmem = pl.BlockSpec(memory_space=pltpu.VMEM)
    small = pltpu.VMEM((heads, length), f32)
    dma = pltpu.SemaphoreType.DMA
    scratch = [
        pltpu.VMEM((n_dp if gather else 1, heads, depth), bf16),
        pltpu.VMEM((heads * HEADDIM, length), bf16),
        pltpu.VMEM((GROUPS, length, NSTATE), f32),
        pltpu.VMEM((GROUPS, 2 * length, NSTATE), bf16),
        pltpu.VMEM((GROUPS, length, length), f32),
        small, small, small, small,
        pltpu.VMEM((heads, length, length), f32),
        pltpu.VMEM((heads, length, length), f32),
        pltpu.VMEM((GROUPS, length, NSTATE), f32),
        small, small, small, small, small,
        pltpu.VMEM((heads * HEADDIM, NSTATE), f32),
        pltpu.VMEM((heads * HEADDIM, NSTATE), f32),
        pltpu.VMEM(hid.shape, bf16),
        pltpu.VMEM(ssm_input.shape[1:], bf16),
        pltpu.VMEM(grad_output.shape[1:], bf16),
        pltpu.VMEM(b_matrix.shape[1:], bf16),
        pltpu.VMEM(c_matrix.shape[1:], bf16),
        pltpu.VMEM((heads * HEADDIM, NSTATE), bf16),
        dma((7,)),
        dma((n_dp,)), dma((n_dp,)), dma((chunks,)), dma((chunks,)),
    ]
    if fuse:
        scratch += [
            pltpu.VMEM((n_dp, length, depth), bf16),
            small,
            pltpu.VMEM((n_dp, heads, length), f32),
            pltpu.VMEM((n_ctx, heads, depth // n_ctx), f32),
            dma((n_dp,)), dma((n_dp,)), dma((n_dp,)), dma((n_dp,)),
            pltpu.VMEM((n_ctx, heads, depth // n_ctx), f32),
            dma((n_ctx,)), dma((n_ctx,)),
            pltpu.VMEM((heads, depth // n_ctx), f32),
            pltpu.VMEM((n_ctx, heads, depth // n_ctx), f32),
            dma((n_ctx,)), dma((n_ctx,)),
        ]
    grad_b, res = pl.pallas_call(
        functools.partial(kernel, (n_dp, n_ctx, gather, fuse)),
        out_shape=(
            jax.ShapeDtypeStruct((length, GROUPS * NSTATE), bf16),
            jax.ShapeDtypeStruct((heads, depth if fuse else length), f32),
        ),
        in_specs=[any_] + [any_ if gather else vmem] + [any_] * 5 + [vmem] * 2 + [pl.BlockSpec(memory_space=pltpu.SMEM)],
        out_specs=(vmem, vmem),
        scratch_shapes=scratch,
        compiler_params=pltpu.CompilerParams(
            collective_id=0, has_side_effects=True, vmem_limit_bytes=63 * 1024 * 1024),
    )(hid, w, ssm_input[0], grad_output[0], b_matrix[0], c_matrix[0],
      stored_states.reshape(heads * HEADDIM, NSTATE), step_bias.reshape(1, heads),
      decay_code.reshape(1, heads), head_group)
    if fuse:
        grad_w = res.T
    else:
        hi = lax.reduce_precision(res, 8, 7)
        both = mm(jnp.concatenate([hi.astype(bf16), (res - hi).astype(bf16)], axis=0), hid)
        part = both[:heads] + both[heads:]
        part = lax.psum_scatter(part, "dp", scatter_dimension=1, tiled=True)
        grad_w = lax.psum(part, "ctx").T
    return grad_b[None], grad_w


def solution(mesh):
    return jax.shard_map(
        functools.partial(body, mesh.shape["dp"], mesh.shape["ctx"]),
        mesh=mesh,
        in_specs=(
            P("dp", "ctx", None),
            P("dp", None),
            P("dp", "ctx", None),
            P("dp", "ctx", None),
            P("dp", "ctx", None),
            P("dp", "ctx", None),
            P("dp", "ctx", None, None, None),
            P(),
            P(),
            P(),
        ),
        out_specs=(P("dp", "ctx", None), P("dp", None)),
        check_vma=False,
    )
```

```python
import functools

import jax
import jax.numpy as jnp
from jax import lax
from jax.experimental import pallas as pl
from jax.experimental.pallas import tpu as pltpu
from jax.sharding import PartitionSpec as P

HEADDIM = 64
NSTATE = 128
GROUPS = 8
CHUNK_HEADS = 2
FUSE_END = True

f32, bf16 = jnp.float32, jnp.bfloat16
MESH = pl.DeviceIdType.MESH
exact = lax.Precision.HIGHEST


def mm(a, b):
    return jnp.dot(a, b, preferred_element_type=f32)


def mm_nt(a, b):
    return lax.dot_general(a, b, (((1,), (1,)), ((), ())), preferred_element_type=f32)


def split(v):
    hi = v.astype(bf16)
    return hi, (v - hi.astype(f32)).astype(bf16)


def kernel(cfg, hid_h, w, x_h, cot_h, b_h, c_h, st_h, bias, code, hg, *rest):
    n_dp, n_ctx, gather, fuse = cfg
    (out_b, out_w), rest = rest[:2], rest[2:]
    (wall, cot_t, bg, cg2, sc, cum_s, last_s, growth_s, elast_s, cumb, stepb, acc,
     row_s, col_s, car_s, end_s, gs_s, send_s, recv_s, hid, x, cot, b, c, st, in_sem,
     w_send, w_recv, ch_send, ch_recv) = rest[:30]
    length = x.shape[0]
    heads = bias.shape[1]
    depth = hid.shape[1] // n_dp
    full_length = length * n_ctx
    dp = lax.axis_index("dp")
    ctx = lax.axis_index("ctx")
    is_last = ctx == n_ctx - 1

    if fuse:
        hall, graw_own, graw_all, part, h_send, h_recv, g_send, g_recv, p_all, p_send, p_recv, mine, final, q_send, q_recv = rest[30:]

    fetches = [
        pltpu.make_async_copy(source, target, in_sem.at[i])
        for i, (source, target) in enumerate(
            ((cot_h, cot), (c_h, c), (b_h, b), (hid_h, hid), (x_h, x), (st_h, st)))
    ]
    own_w = pltpu.make_async_copy(w, wall.at[dp if gather else 0], in_sem.at[6])
    barrier = pltpu.get_barrier_semaphore()
    if gather or fuse:
        for r in range(1, n_dp):
            pl.semaphore_signal(barrier, inc=1, device_id=(lax.rem(dp + r, n_dp), ctx), device_id_type=MESH)
    for r in range(1, n_ctx):
        pl.semaphore_signal(barrier, inc=1, device_id=(dp, lax.rem(ctx + r, n_ctx)), device_id_type=MESH)

    ri = lax.broadcasted_iota(jnp.int32, (heads, heads), 0)
    ci = lax.broadcasted_iota(jnp.int32, (heads, heads), 1)
    eye = ri == ci
    if gather:
        own_w.start()
    for fetch in fetches:
        fetch.start()
    pl.semaphore_wait(barrier, (n_dp - 1 if gather or fuse else 0) + n_ctx - 1)

    def w_copy(r, peer, slot):
        return pltpu.make_async_remote_copy(
            src_ref=w, dst_ref=wall.at[slot], send_sem=w_send.at[r], recv_sem=w_recv.at[r],
            device_id=(peer, ctx), device_id_type=MESH)

    def h_copy(r, peer, slot):
        return pltpu.make_async_remote_copy(
            src_ref=hid_h.at[:, pl.ds(pl.multiple_of(peer * depth, depth), depth)], dst_ref=hall.at[slot],
            send_sem=h_send.at[r], recv_sem=h_recv.at[r], device_id=(peer, ctx), device_id_type=MESH)

    if gather:
        for r in range(1, n_dp):
            w_copy(r, lax.rem(dp + r, n_dp), dp).start()
    if fuse:
        for r in range(1, n_dp):
            h_copy(r, lax.rem(dp + r, n_dp), dp).start()

    fetches[0].wait()
    for k in range(x.shape[1] // 128):
        cot_t[pl.ds(128 * k, 128), :] = cot[:, pl.ds(128 * k, 128)].T
    fetches[1].wait()
    fetches[2].wait()
    for g in range(GROUPS):
        b_g = b[:, pl.ds(NSTATE * g, NSTATE)]
        c_g = c[:, pl.ds(NSTATE * g, NSTATE)]
        bg[g] = b_g.astype(f32)
        cg2[g, :length, :] = c_g
        cg2[g, length:, :] = c_g
        sc[g] = mm_nt(b_g, c_g)
    acc[...] = jnp.zeros_like(acc)

    @pl.when(is_last)
    def _():
        recv_s[...] = jnp.zeros_like(recv_s)

    bias_c = jnp.sum(jnp.where(eye, bias[...], 0.0), axis=1, keepdims=True)
    rate_c = jnp.sum(jnp.where(eye, code[...].astype(f32), 0.0), axis=1, keepdims=True) / (256.0 * full_length)

    fetches[3].wait()
    if fuse:
        hall[dp] = hid[:, pl.ds(pl.multiple_of(dp * depth, depth), depth)]
    if gather:
        own_w.wait()
        for r in range(1, n_dp):
            w_copy(r, lax.rem(dp + r, n_dp), lax.rem(dp - r + n_dp, n_dp)).wait_recv()
    proj = jnp.zeros((heads, length), f32)
    for d in range(n_dp):
        proj = proj + mm_nt(wall[d] if gather else w[d], hid[:, d * depth:(d + 1) * depth])
    shifted = proj + bias_c
    timestep = jnp.maximum(shifted, 0.0) + jnp.log1p(jnp.exp(-jnp.abs(shifted)))
    gain = 1.0 / (1.0 + jnp.exp(-shifted))
    rows = lax.broadcasted_iota(jnp.int32, (length, length), 0)
    cols = lax.broadcasted_iota(jnp.int32, (length, length), 1)
    causal = rows <= cols
    cum = jnp.dot(-rate_c * timestep, causal.astype(f32), precision=exact, preferred_element_type=f32)
    last = jnp.broadcast_to(cum[:, length - 1:length], (heads, length))
    cum_s[...] = cum
    last_s[...] = last
    growth_s[...] = jnp.exp(cum)
    elast_s[...] = jnp.exp(last)

    def chain(k):
        span = pl.ds(pl.multiple_of(k * HEADDIM, HEADDIM), HEADDIM)
        return pltpu.make_async_remote_copy(
            src_ref=send_s.at[span], dst_ref=recv_s.at[span], send_sem=ch_send.at[k], recv_sem=ch_recv.at[k],
            device_id=(dp, lax.rem(ctx - 1 + n_ctx, n_ctx)), device_id_type=MESH)

    def own_chunk(k, carry):
        for e in range(CHUNK_HEADS):
            h = k * CHUNK_HEADS + e
            span = pl.ds(pl.multiple_of(h * HEADDIM, HEADDIM), HEADDIM)
            weighted = cot_t[span, :].astype(f32) * growth_s[pl.ds(h, 1), :]
            both = mm(jnp.concatenate(split(weighted), axis=0), cg2[hg[h], :length, :])
            send_s[span, :] = both[:HEADDIM] + both[HEADDIM:]

            @pl.when(is_last)
            def _():
                chain(h).start()

        return carry

    chunks = heads // CHUNK_HEADS
    lax.fori_loop(0, chunks, own_chunk, 0)

    both_t = jnp.concatenate([cum, timestep, jnp.zeros((length - 2 * heads, length), f32)], axis=0).T
    for h in range(heads):
        cumb[h] = jnp.broadcast_to(both_t[:, h:h + 1], (length, length))
        stepb[h] = jnp.broadcast_to(both_t[:, heads + h:heads + h + 1], (length, length))

    low_lanes = lax.broadcasted_iota(jnp.int32, (length, 128), 1) < HEADDIM
    ones = jnp.ones((8, 256), bf16)

    def main_chunk(k, carry):
        for e in range(CHUNK_HEADS):
            h = k * CHUNK_HEADS + e
            span = pl.ds(pl.multiple_of(h * HEADDIM, HEADDIM), HEADDIM)

            @pl.when(ctx < n_ctx - 1)
            def _():
                chain(h).wait_recv()

            @pl.when(jnp.logical_and(ctx < n_ctx - 1, ctx > 0))
            def _():
                send_s[span, :] = send_s[span, :] + elast_s[pl.ds(h, 1), :] * recv_s[span, :]
                chain(h).start()

        grads = []
        for q in range(CHUNK_HEADS // 2):
            pair = k * (CHUNK_HEADS // 2) + q
            lanes = pl.ds(pl.multiple_of(pair * 128, 128), 128)
            xp = x[:, lanes]
            cp = cot[:, lanes]
            incoming = recv_s[lanes, :]
            rhs = jnp.concatenate(split(incoming), axis=0)
            product_state = incoming * st[lanes, :].astype(f32)
            for e in range(2):
                h = pair * 2 + e
                g = hg[h]
                row = pl.ds(h, 1)
                span = pl.ds(pl.multiple_of(h * HEADDIM, HEADDIM), HEADDIM)
                mask = low_lanes if e == 0 else jnp.logical_not(low_lanes)
                xm = jnp.where(mask, xp, jnp.zeros_like(xp))
                c2 = cg2[g]
                cum_h = cumb[h]
                step_h = stepb[h]
                gaps = cum_s[row, :] - cum_h
                decay = jnp.where(causal, jnp.exp(jnp.where(causal, gaps, 0.0)), 0.0)
                m = decay * mm_nt(xm, cp)
                scored = m * sc[g]
                x_state = mm(jnp.concatenate([xm, xm], axis=1), rhs)
                to_end = jnp.exp(last_s[row, :] - cum_h)
                grads.append((h, step_h * (mm(jnp.concatenate(split(m), axis=1), c2) + to_end * x_state)))
                row_s[row, :] = jnp.sum(scored * step_h, axis=0, keepdims=True)
                col_s[row, :] = mm_nt(ones, jnp.concatenate(split(scored), axis=1))[:1]
                end_s[row, :] = mm_nt(ones, jnp.concatenate(split(x_state * bg[g]), axis=1))[:1]
                carried = mm_nt(st[span, :], c2[:length])
                car_s[row, :] = jnp.sum(cot_t[span, :].astype(f32) * carried, axis=0, keepdims=True)
                gs_s[row, :] = jnp.sum(
                    product_state[e * HEADDIM:(e + 1) * HEADDIM], axis=0, keepdims=True)
        for g in range(GROUPS):
            total = acc[g]
            for h, value in grads:
                total = total + jnp.where(hg[h] == g, 1.0, 0.0) * value
            acc[g] = total
        return carry

    fetches[4].wait()
    fetches[5].wait()
    lax.fori_loop(0, chunks, main_chunk, 0)

    col = col_s[...]
    end_plain = jnp.exp(last_s[...] - cum_s[...]) * end_s[...]
    end_term = end_plain * timestep
    grad_cum = row_s[...] - col * timestep + growth_s[...] * car_s[...] - end_term
    end_total = jnp.sum(end_term, axis=1, keepdims=True) + elast_s[:, :1] * jnp.sum(gs_s[...], axis=1, keepdims=True)
    lane = lax.broadcasted_iota(jnp.int32, (heads, length), 1)
    grad_cum = grad_cum + jnp.where(lane == length - 1, end_total, 0.0)
    backward = jnp.dot(grad_cum, (rows >= cols).astype(f32), precision=exact, preferred_element_type=f32)
    grad_raw = (col + end_plain - rate_c * backward) * gain

    def g_copy(r, peer, slot):
        return pltpu.make_async_remote_copy(
            src_ref=graw_own, dst_ref=graw_all.at[slot], send_sem=g_send.at[r], recv_sem=g_recv.at[r],
            device_id=(peer, ctx), device_id_type=MESH)

    def p_copy(r, peer, slot):
        return pltpu.make_async_remote_copy(
            src_ref=part.at[peer], dst_ref=p_all.at[slot], send_sem=p_send.at[r], recv_sem=p_recv.at[r],
            device_id=(dp, peer), device_id_type=MESH)

    def q_copy(r, peer, slot):
        return pltpu.make_async_remote_copy(
            src_ref=mine, dst_ref=final.at[slot], send_sem=q_send.at[r], recv_sem=q_recv.at[r],
            device_id=(dp, peer), device_id_type=MESH)

    if fuse:
        graw_own[...] = grad_raw
        for r in range(1, n_dp):
            g_copy(r, lax.rem(dp + r, n_dp), dp).start()
        graw_all[dp] = grad_raw
    else:
        out_w[...] = grad_raw

    for g in range(GROUPS):
        out_b[:, pl.ds(NSTATE * g, NSTATE)] = acc[g].astype(bf16)

    if fuse:
        total = jnp.zeros((2 * heads, depth), f32)
        for r in range(1, n_dp):
            source = lax.rem(dp - r + n_dp, n_dp)
            h_copy(r, lax.rem(dp + r, n_dp), source).wait_recv()
        for r in range(1, n_dp):
            source = lax.rem(dp - r + n_dp, n_dp)
            g_copy(r, lax.rem(dp + r, n_dp), source).wait_recv()
        for d in range(n_dp):
            total = total + mm(jnp.concatenate(split(graw_all[d]), axis=0), hall[d])
        total = total[:heads] + total[heads:]
        piece = depth // n_ctx
        for d in range(n_ctx):
            part[d] = total[:, d * piece:(d + 1) * piece]
        for r in range(1, n_ctx):
            p_copy(r, lax.rem(ctx + r, n_ctx), ctx).start()
        p_all[ctx] = part[ctx]
        for r in range(1, n_ctx):
            p_copy(r, lax.rem(ctx + r, n_ctx), lax.rem(ctx - r + n_ctx, n_ctx)).wait_recv()
        summed = p_all[0]
        for d in range(1, n_ctx):
            summed = summed + p_all[d]
        mine[...] = summed
        for r in range(1, n_ctx):
            q_copy(r, lax.rem(ctx + r, n_ctx), ctx).start()
        final[ctx] = summed
        for r in range(1, n_ctx):
            q_copy(r, lax.rem(ctx + r, n_ctx), lax.rem(ctx - r + n_ctx, n_ctx)).wait_recv()
        for d in range(n_ctx):
            out_w[:, d * piece:(d + 1) * piece] = final[d]
        for r in range(1, n_ctx):
            p_copy(r, lax.rem(ctx + r, n_ctx), ctx).wait_send()
            q_copy(r, lax.rem(ctx + r, n_ctx), ctx).wait_send()
        for r in range(1, n_dp):
            h_copy(r, lax.rem(dp + r, n_dp), dp).wait_send()
            g_copy(r, lax.rem(dp + r, n_dp), dp).wait_send()

    if gather:
        for r in range(1, n_dp):
            w_copy(r, lax.rem(dp + r, n_dp), dp).wait_send()

    @pl.when(ctx > 0)
    def _():
        def drain(k, carry):
            chain(k).wait_send()
            return carry

        lax.fori_loop(0, heads, drain, 0)


def body(n_dp, n_ctx, hidden, dt_weight, ssm_input, grad_output, b_matrix, c_matrix,
         stored_states, step_bias, decay_code, head_group):
    length, width = hidden.shape[1:]
    depth = dt_weight.shape[0]
    heads = step_bias.shape[0]
    gather = depth % 128 == 0
    fuse = FUSE_END and depth % (128 * n_ctx) == 0
    hid = hidden[0]
    if gather:
        w = dt_weight.T
    else:
        w = lax.all_gather(dt_weight.T, "dp", axis=0, tiled=False)
    any_ = pl.BlockSpec(memory_space=pltpu.HBM)
    vmem = pl.BlockSpec(memory_space=pltpu.VMEM)
    small = pltpu.VMEM((heads, length), f32)
    dma = pltpu.SemaphoreType.DMA
    scratch = [
        pltpu.VMEM((n_dp if gather else 1, heads, depth), bf16),
        pltpu.VMEM((heads * HEADDIM, length), bf16),
        pltpu.VMEM((GROUPS, length, NSTATE), f32),
        pltpu.VMEM((GROUPS, 2 * length, NSTATE), bf16),
        pltpu.VMEM((GROUPS, length, length), f32),
        small, small, small, small,
        pltpu.VMEM((heads, length, length), f32),
        pltpu.VMEM((heads, length, length), f32),
        pltpu.VMEM((GROUPS, length, NSTATE), f32),
        small, small, small, small, small,
        pltpu.VMEM((heads * HEADDIM, NSTATE), f32),
        pltpu.VMEM((heads * HEADDIM, NSTATE), f32),
        pltpu.VMEM(hid.shape, bf16),
        pltpu.VMEM(ssm_input.shape[1:], bf16),
        pltpu.VMEM(grad_output.shape[1:], bf16),
        pltpu.VMEM(b_matrix.shape[1:], bf16),
        pltpu.VMEM(c_matrix.shape[1:], bf16),
        pltpu.VMEM((heads * HEADDIM, NSTATE), bf16),
        dma((7,)),
        dma((n_dp,)), dma((n_dp,)), dma((heads,)), dma((heads,)),
    ]
    if fuse:
        scratch += [
            pltpu.VMEM((n_dp, length, depth), bf16),
            small,
            pltpu.VMEM((n_dp, heads, length), f32),
            pltpu.VMEM((n_ctx, heads, depth // n_ctx), f32),
            dma((n_dp,)), dma((n_dp,)), dma((n_dp,)), dma((n_dp,)),
            pltpu.VMEM((n_ctx, heads, depth // n_ctx), f32),
            dma((n_ctx,)), dma((n_ctx,)),
            pltpu.VMEM((heads, depth // n_ctx), f32),
            pltpu.VMEM((n_ctx, heads, depth // n_ctx), f32),
            dma((n_ctx,)), dma((n_ctx,)),
        ]
    grad_b, res = pl.pallas_call(
        functools.partial(kernel, (n_dp, n_ctx, gather, fuse)),
        out_shape=(
            jax.ShapeDtypeStruct((length, GROUPS * NSTATE), bf16),
            jax.ShapeDtypeStruct((heads, depth if fuse else length), f32),
        ),
        in_specs=[any_] + [any_ if gather else vmem] + [any_] * 5 + [vmem] * 2 + [pl.BlockSpec(memory_space=pltpu.SMEM)],
        out_specs=(vmem, vmem),
        scratch_shapes=scratch,
        compiler_params=pltpu.CompilerParams(
            collective_id=0, has_side_effects=True, vmem_limit_bytes=63 * 1024 * 1024),
    )(hid, w, ssm_input[0], grad_output[0], b_matrix[0], c_matrix[0],
      stored_states.reshape(heads * HEADDIM, NSTATE), step_bias.reshape(1, heads),
      decay_code.reshape(1, heads), head_group)
    if fuse:
        grad_w = res.T
    else:
        hi = lax.reduce_precision(res, 8, 7)
        both = mm(jnp.concatenate([hi.astype(bf16), (res - hi).astype(bf16)], axis=0), hid)
        part = both[:heads] + both[heads:]
        part = lax.psum_scatter(part, "dp", scatter_dimension=1, tiled=True)
        grad_w = lax.psum(part, "ctx").T
    return grad_b[None], grad_w


def solution(mesh):
    return jax.shard_map(
        functools.partial(body, mesh.shape["dp"], mesh.shape["ctx"]),
        mesh=mesh,
        in_specs=(
            P("dp", "ctx", None),
            P("dp", None),
            P("dp", "ctx", None),
            P("dp", "ctx", None),
            P("dp", "ctx", None),
            P("dp", "ctx", None),
            P("dp", "ctx", None, None, None),
            P(),
            P(),
            P(),
        ),
        out_specs=(P("dp", "ctx", None), P("dp", None)),
        check_vma=False,
    )
```

```python
import functools

import jax
import jax.numpy as jnp
from jax import lax
from jax.experimental import pallas as pl
from jax.experimental.pallas import tpu as pltpu
from jax.sharding import PartitionSpec as P

HEADDIM = 64
NSTATE = 128
GROUPS = 8
CHUNK_HEADS = 2
FUSE_END = True

f32, bf16 = jnp.float32, jnp.bfloat16
MESH = pl.DeviceIdType.MESH
exact = lax.Precision.HIGHEST


def mm(a, b):
    return jnp.dot(a, b, preferred_element_type=f32)


def mm_nt(a, b):
    return lax.dot_general(a, b, (((1,), (1,)), ((), ())), preferred_element_type=f32)


def split(v):
    hi = v.astype(bf16)
    return hi, (v - hi.astype(f32)).astype(bf16)


def kernel(cfg, hid_h, w, x_h, cot_h, b_h, c_h, st_h, bias, code, hg, *rest):
    n_dp, n_ctx, gather, fuse = cfg
    (out_b, out_w), rest = rest[:2], rest[2:]
    (wall, cot_t, bg, cg2, sc, cum_s, last_s, growth_s, elast_s, cumb, stepb, acc,
     row_s, col_s, car_s, end_s, gs_s, send_s, recv_s, hid, x, cot, b, c, st, in_sem,
     w_send, w_recv, ch_send, ch_recv) = rest[:30]
    length = x.shape[0]
    heads = bias.shape[1]
    depth = hid.shape[1] // n_dp
    full_length = length * n_ctx
    dp = lax.axis_index("dp")
    ctx = lax.axis_index("ctx")
    is_last = ctx == n_ctx - 1

    if fuse:
        hall, graw_own, graw_all, part, h_send, h_recv, g_send, g_recv, p_all, p_send, p_recv, mine, final, q_send, q_recv = rest[30:]

    fetches = [
        pltpu.make_async_copy(source, target, in_sem.at[i])
        for i, (source, target) in enumerate(
            ((cot_h, cot), (c_h, c), (b_h, b), (hid_h, hid), (x_h, x), (st_h, st)))
    ]
    own_w = pltpu.make_async_copy(w, wall.at[dp if gather else 0], in_sem.at[6])
    barrier = pltpu.get_barrier_semaphore()
    if gather or fuse:
        for r in range(1, n_dp):
            pl.semaphore_signal(barrier, inc=1, device_id=(lax.rem(dp + r, n_dp), ctx), device_id_type=MESH)
    for r in range(1, n_ctx):
        pl.semaphore_signal(barrier, inc=1, device_id=(dp, lax.rem(ctx + r, n_ctx)), device_id_type=MESH)

    ri = lax.broadcasted_iota(jnp.int32, (heads, heads), 0)
    ci = lax.broadcasted_iota(jnp.int32, (heads, heads), 1)
    eye = ri == ci
    if gather:
        own_w.start()
    for fetch in fetches:
        fetch.start()
    pl.semaphore_wait(barrier, (n_dp - 1 if gather or fuse else 0) + n_ctx - 1)

    def w_copy(r, peer, slot):
        return pltpu.make_async_remote_copy(
            src_ref=w, dst_ref=wall.at[slot], send_sem=w_send.at[r], recv_sem=w_recv.at[r],
            device_id=(peer, ctx), device_id_type=MESH)

    def h_copy(r, peer, slot):
        return pltpu.make_async_remote_copy(
            src_ref=hid_h.at[:, pl.ds(pl.multiple_of(peer * depth, depth), depth)], dst_ref=hall.at[slot],
            send_sem=h_send.at[r], recv_sem=h_recv.at[r], device_id=(peer, ctx), device_id_type=MESH)

    if gather:
        for r in range(1, n_dp):
            w_copy(r, lax.rem(dp + r, n_dp), dp).start()

    fetches[0].wait()
    for k in range(x.shape[1] // 128):
        cot_t[pl.ds(128 * k, 128), :] = cot[:, pl.ds(128 * k, 128)].T
    fetches[1].wait()
    fetches[2].wait()
    for g in range(GROUPS):
        b_g = b[:, pl.ds(NSTATE * g, NSTATE)]
        c_g = c[:, pl.ds(NSTATE * g, NSTATE)]
        bg[g] = b_g.astype(f32)
        cg2[g, :length, :] = c_g
        cg2[g, length:, :] = c_g
        sc[g] = mm_nt(b_g, c_g)
    acc[...] = jnp.zeros_like(acc)

    @pl.when(is_last)
    def _():
        recv_s[...] = jnp.zeros_like(recv_s)

    bias_c = jnp.sum(jnp.where(eye, bias[...], 0.0), axis=1, keepdims=True)
    rate_c = jnp.sum(jnp.where(eye, code[...].astype(f32), 0.0), axis=1, keepdims=True) / (256.0 * full_length)

    fetches[3].wait()
    if fuse:
        hall[dp] = hid[:, pl.ds(pl.multiple_of(dp * depth, depth), depth)]
    if gather:
        own_w.wait()
        for r in range(1, n_dp):
            w_copy(r, lax.rem(dp + r, n_dp), lax.rem(dp - r + n_dp, n_dp)).wait_recv()
    if fuse:
        for r in range(1, n_dp):
            h_copy(r, lax.rem(dp + r, n_dp), dp).start()
    proj = jnp.zeros((heads, length), f32)
    for d in range(n_dp):
        proj = proj + mm_nt(wall[d] if gather else w[d], hid[:, d * depth:(d + 1) * depth])
    shifted = proj + bias_c
    timestep = jnp.maximum(shifted, 0.0) + jnp.log1p(jnp.exp(-jnp.abs(shifted)))
    gain = 1.0 / (1.0 + jnp.exp(-shifted))
    rows = lax.broadcasted_iota(jnp.int32, (length, length), 0)
    cols = lax.broadcasted_iota(jnp.int32, (length, length), 1)
    causal = rows <= cols
    cum = jnp.dot(-rate_c * timestep, causal.astype(f32), precision=exact, preferred_element_type=f32)
    last = jnp.broadcast_to(cum[:, length - 1:length], (heads, length))
    cum_s[...] = cum
    last_s[...] = last
    growth_s[...] = jnp.exp(cum)
    elast_s[...] = jnp.exp(last)

    def chain(k):
        span = pl.ds(pl.multiple_of(k * (CHUNK_HEADS * HEADDIM), CHUNK_HEADS * HEADDIM), CHUNK_HEADS * HEADDIM)
        return pltpu.make_async_remote_copy(
            src_ref=send_s.at[span], dst_ref=recv_s.at[span], send_sem=ch_send.at[k], recv_sem=ch_recv.at[k],
            device_id=(dp, lax.rem(ctx - 1 + n_ctx, n_ctx)), device_id_type=MESH)

    def own_chunk(k, carry):
        for e in range(CHUNK_HEADS):
            h = k * CHUNK_HEADS + e
            span = pl.ds(pl.multiple_of(h * HEADDIM, HEADDIM), HEADDIM)
            weighted = cot_t[span, :].astype(f32) * growth_s[pl.ds(h, 1), :]
            both = mm(jnp.concatenate(split(weighted), axis=0), cg2[hg[h], :length, :])
            send_s[span, :] = both[:HEADDIM] + both[HEADDIM:]

        @pl.when(is_last)
        def _():
            chain(k).start()

        return carry

    chunks = heads // CHUNK_HEADS
    lax.fori_loop(0, chunks, own_chunk, 0)

    both_t = jnp.concatenate([cum, timestep, jnp.zeros((length - 2 * heads, length), f32)], axis=0).T
    for h in range(heads):
        cumb[h] = jnp.broadcast_to(both_t[:, h:h + 1], (length, length))
        stepb[h] = jnp.broadcast_to(both_t[:, heads + h:heads + h + 1], (length, length))

    low_lanes = lax.broadcasted_iota(jnp.int32, (length, 128), 1) < HEADDIM
    ones = jnp.ones((8, 256), bf16)

    def main_chunk(k, carry):
        @pl.when(ctx < n_ctx - 1)
        def _():
            chain(k).wait_recv()

        @pl.when(jnp.logical_and(ctx < n_ctx - 1, ctx > 0))
        def _():
            for e in range(CHUNK_HEADS):
                h = k * CHUNK_HEADS + e
                span = pl.ds(pl.multiple_of(h * HEADDIM, HEADDIM), HEADDIM)
                send_s[span, :] = send_s[span, :] + elast_s[pl.ds(h, 1), :] * recv_s[span, :]
            chain(k).start()

        grads = []
        for q in range(CHUNK_HEADS // 2):
            pair = k * (CHUNK_HEADS // 2) + q
            lanes = pl.ds(pl.multiple_of(pair * 128, 128), 128)
            xp = x[:, lanes]
            cp = cot[:, lanes]
            incoming = recv_s[lanes, :]
            rhs = jnp.concatenate(split(incoming), axis=0)
            product_state = incoming * st[lanes, :].astype(f32)
            for e in range(2):
                h = pair * 2 + e
                g = hg[h]
                row = pl.ds(h, 1)
                span = pl.ds(pl.multiple_of(h * HEADDIM, HEADDIM), HEADDIM)
                mask = low_lanes if e == 0 else jnp.logical_not(low_lanes)
                xm = jnp.where(mask, xp, jnp.zeros_like(xp))
                c2 = cg2[g]
                cum_h = cumb[h]
                step_h = stepb[h]
                gaps = cum_s[row, :] - cum_h
                decay = jnp.where(causal, jnp.exp(jnp.where(causal, gaps, 0.0)), 0.0)
                m = decay * mm_nt(xm, cp)
                scored = m * sc[g]
                x_state = mm(jnp.concatenate([xm, xm], axis=1), rhs)
                to_end = jnp.exp(last_s[row, :] - cum_h)
                grads.append((h, step_h * (mm(jnp.concatenate(split(m), axis=1), c2) + to_end * x_state)))
                row_s[row, :] = jnp.sum(scored * step_h, axis=0, keepdims=True)
                col_s[row, :] = mm_nt(ones, jnp.concatenate(split(scored), axis=1))[:1]
                end_s[row, :] = mm_nt(ones, jnp.concatenate(split(x_state * bg[g]), axis=1))[:1]
                carried = mm_nt(st[span, :], c2[:length])
                car_s[row, :] = jnp.sum(cot_t[span, :].astype(f32) * carried, axis=0, keepdims=True)
                gs_s[row, :] = jnp.sum(
                    product_state[e * HEADDIM:(e + 1) * HEADDIM], axis=0, keepdims=True)
        for g in range(GROUPS):
            total = acc[g]
            for h, value in grads:
                total = total + jnp.where(hg[h] == g, 1.0, 0.0) * value
            acc[g] = total
        return carry

    fetches[4].wait()
    fetches[5].wait()
    lax.fori_loop(0, chunks, main_chunk, 0)

    col = col_s[...]
    end_plain = jnp.exp(last_s[...] - cum_s[...]) * end_s[...]
    end_term = end_plain * timestep
    grad_cum = row_s[...] - col * timestep + growth_s[...] * car_s[...] - end_term
    end_total = jnp.sum(end_term, axis=1, keepdims=True) + elast_s[:, :1] * jnp.sum(gs_s[...], axis=1, keepdims=True)
    lane = lax.broadcasted_iota(jnp.int32, (heads, length), 1)
    grad_cum = grad_cum + jnp.where(lane == length - 1, end_total, 0.0)
    backward = jnp.dot(grad_cum, (rows >= cols).astype(f32), precision=exact, preferred_element_type=f32)
    grad_raw = (col + end_plain - rate_c * backward) * gain

    def g_copy(r, peer, slot):
        return pltpu.make_async_remote_copy(
            src_ref=graw_own, dst_ref=graw_all.at[slot], send_sem=g_send.at[r], recv_sem=g_recv.at[r],
            device_id=(peer, ctx), device_id_type=MESH)

    def p_copy(r, peer, slot):
        return pltpu.make_async_remote_copy(
            src_ref=part.at[peer], dst_ref=p_all.at[slot], send_sem=p_send.at[r], recv_sem=p_recv.at[r],
            device_id=(dp, peer), device_id_type=MESH)

    def q_copy(r, peer, slot):
        return pltpu.make_async_remote_copy(
            src_ref=mine, dst_ref=final.at[slot], send_sem=q_send.at[r], recv_sem=q_recv.at[r],
            device_id=(dp, peer), device_id_type=MESH)

    if fuse:
        graw_own[...] = grad_raw
        for r in range(1, n_dp):
            g_copy(r, lax.rem(dp + r, n_dp), dp).start()
        graw_all[dp] = grad_raw
    else:
        out_w[...] = grad_raw

    for g in range(GROUPS):
        out_b[:, pl.ds(NSTATE * g, NSTATE)] = acc[g].astype(bf16)

    if fuse:
        total = jnp.zeros((2 * heads, depth), f32)
        for r in range(1, n_dp):
            source = lax.rem(dp - r + n_dp, n_dp)
            h_copy(r, lax.rem(dp + r, n_dp), source).wait_recv()
        for r in range(1, n_dp):
            source = lax.rem(dp - r + n_dp, n_dp)
            g_copy(r, lax.rem(dp + r, n_dp), source).wait_recv()
        for d in range(n_dp):
            total = total + mm(jnp.concatenate(split(graw_all[d]), axis=0), hall[d])
        total = total[:heads] + total[heads:]
        piece = depth // n_ctx
        for d in range(n_ctx):
            part[d] = total[:, d * piece:(d + 1) * piece]
        for r in range(1, n_ctx):
            p_copy(r, lax.rem(ctx + r, n_ctx), ctx).start()
        p_all[ctx] = part[ctx]
        for r in range(1, n_ctx):
            p_copy(r, lax.rem(ctx + r, n_ctx), lax.rem(ctx - r + n_ctx, n_ctx)).wait_recv()
        summed = p_all[0]
        for d in range(1, n_ctx):
            summed = summed + p_all[d]
        mine[...] = summed
        for r in range(1, n_ctx):
            q_copy(r, lax.rem(ctx + r, n_ctx), ctx).start()
        final[ctx] = summed
        for r in range(1, n_ctx):
            q_copy(r, lax.rem(ctx + r, n_ctx), lax.rem(ctx - r + n_ctx, n_ctx)).wait_recv()
        for d in range(n_ctx):
            out_w[:, d * piece:(d + 1) * piece] = final[d]
        for r in range(1, n_ctx):
            p_copy(r, lax.rem(ctx + r, n_ctx), ctx).wait_send()
            q_copy(r, lax.rem(ctx + r, n_ctx), ctx).wait_send()
        for r in range(1, n_dp):
            h_copy(r, lax.rem(dp + r, n_dp), dp).wait_send()
            g_copy(r, lax.rem(dp + r, n_dp), dp).wait_send()

    if gather:
        for r in range(1, n_dp):
            w_copy(r, lax.rem(dp + r, n_dp), dp).wait_send()

    @pl.when(ctx > 0)
    def _():
        def drain(k, carry):
            chain(k).wait_send()
            return carry

        lax.fori_loop(0, chunks, drain, 0)


def body(n_dp, n_ctx, hidden, dt_weight, ssm_input, grad_output, b_matrix, c_matrix,
         stored_states, step_bias, decay_code, head_group):
    length, width = hidden.shape[1:]
    depth = dt_weight.shape[0]
    heads = step_bias.shape[0]
    gather = depth % 128 == 0
    fuse = FUSE_END and depth % (128 * n_ctx) == 0
    hid = hidden[0]
    if gather:
        w = dt_weight.T
    else:
        w = lax.all_gather(dt_weight.T, "dp", axis=0, tiled=False)
    chunks = heads // CHUNK_HEADS
    any_ = pl.BlockSpec(memory_space=pltpu.HBM)
    vmem = pl.BlockSpec(memory_space=pltpu.VMEM)
    small = pltpu.VMEM((heads, length), f32)
    dma = pltpu.SemaphoreType.DMA
    scratch = [
        pltpu.VMEM((n_dp if gather else 1, heads, depth), bf16),
        pltpu.VMEM((heads * HEADDIM, length), bf16),
        pltpu.VMEM((GROUPS, length, NSTATE), f32),
        pltpu.VMEM((GROUPS, 2 * length, NSTATE), bf16),
        pltpu.VMEM((GROUPS, length, length), f32),
        small, small, small, small,
        pltpu.VMEM((heads, length, length), f32),
        pltpu.VMEM((heads, length, length), f32),
        pltpu.VMEM((GROUPS, length, NSTATE), f32),
        small, small, small, small, small,
        pltpu.VMEM((heads * HEADDIM, NSTATE), f32),
        pltpu.VMEM((heads * HEADDIM, NSTATE), f32),
        pltpu.VMEM(hid.shape, bf16),
        pltpu.VMEM(ssm_input.shape[1:], bf16),
        pltpu.VMEM(grad_output.shape[1:], bf16),
        pltpu.VMEM(b_matrix.shape[1:], bf16),
        pltpu.VMEM(c_matrix.shape[1:], bf16),
        pltpu.VMEM((heads * HEADDIM, NSTATE), bf16),
        dma((7,)),
        dma((n_dp,)), dma((n_dp,)), dma((chunks,)), dma((chunks,)),
    ]
    if fuse:
        scratch += [
            pltpu.VMEM((n_dp, length, depth), bf16),
            small,
            pltpu.VMEM((n_dp, heads, length), f32),
            pltpu.VMEM((n_ctx, heads, depth // n_ctx), f32),
            dma((n_dp,)), dma((n_dp,)), dma((n_dp,)), dma((n_dp,)),
            pltpu.VMEM((n_ctx, heads, depth // n_ctx), f32),
            dma((n_ctx,)), dma((n_ctx,)),
            pltpu.VMEM((heads, depth // n_ctx), f32),
            pltpu.VMEM((n_ctx, heads, depth // n_ctx), f32),
            dma((n_ctx,)), dma((n_ctx,)),
        ]
    grad_b, res = pl.pallas_call(
        functools.partial(kernel, (n_dp, n_ctx, gather, fuse)),
        out_shape=(
            jax.ShapeDtypeStruct((length, GROUPS * NSTATE), bf16),
            jax.ShapeDtypeStruct((heads, depth if fuse else length), f32),
        ),
        in_specs=[any_] + [any_ if gather else vmem] + [any_] * 5 + [vmem] * 2 + [pl.BlockSpec(memory_space=pltpu.SMEM)],
        out_specs=(vmem, vmem),
        scratch_shapes=scratch,
        compiler_params=pltpu.CompilerParams(
            collective_id=0, has_side_effects=True, vmem_limit_bytes=63 * 1024 * 1024),
    )(hid, w, ssm_input[0], grad_output[0], b_matrix[0], c_matrix[0],
      stored_states.reshape(heads * HEADDIM, NSTATE), step_bias.reshape(1, heads),
      decay_code.reshape(1, heads), head_group)
    if fuse:
        grad_w = res.T
    else:
        hi = lax.reduce_precision(res, 8, 7)
        both = mm(jnp.concatenate([hi.astype(bf16), (res - hi).astype(bf16)], axis=0), hid)
        part = both[:heads] + both[heads:]
        part = lax.psum_scatter(part, "dp", scatter_dimension=1, tiled=True)
        grad_w = lax.psum(part, "ctx").T
    return grad_b[None], grad_w


def solution(mesh):
    return jax.shard_map(
        functools.partial(body, mesh.shape["dp"], mesh.shape["ctx"]),
        mesh=mesh,
        in_specs=(
            P("dp", "ctx", None),
            P("dp", None),
            P("dp", "ctx", None),
            P("dp", "ctx", None),
            P("dp", "ctx", None),
            P("dp", "ctx", None),
            P("dp", "ctx", None, None, None),
            P(),
            P(),
            P(),
        ),
        out_specs=(P("dp", "ctx", None), P("dp", None)),
        check_vma=False,
    )
```
